32 devices in a mesh: wide: 8 (over z, x), slab: 4 (over y, core).
Axes of the slice: x: 2, y: 2, z: 4, core: 2. Of those that a mesh axis runs over, the one named last changes fastest.
Arguments:
- fields: float32 [4, 512, 64, 512], P(None, 'slab', 'wide'), may hold values from -60 to 60
- start_basis: float32 [512, 128], replicated, may hold values from -6 to 6
Outputs:
- core_tensor: float32 [4, 512, 64, 128], P(None, None, ('wide', 'slab'))
The draws below stay inside these ranges and needn't reach their ends.
All inputs are finite; a program needn't handle non-finite values.
Results may differ from the reference program's by a relative error of at most 0.0003.
Values sent between devices are 32-bit elements; how exact they have to be, the bound alone decides.
No kernel may reach another device: no remote copies, remote signals or barrier semaphores. Data moves between devices by JAX's collectives and lax.ppermute only.
A program may use at most 64 MiB of HBM per device.

```python
import jax
import jax.numpy as jnp
from jax import lax

N1 = 512
RANK = 128
NV = 4
SWEEPS = 4
N2 = 512
N3 = 64


def draw_fields(key, part):
    keys = jax.random.split(key, 4)
    scales = jnp.exp(jax.random.uniform(keys[0], (N1,), jnp.float32, 0.0, 1.7918))
    noise = jnp.clip(jax.random.normal(keys[1], (NV, N2, N3, N1), jnp.float32), -5.0, 5.0)
    loads = jnp.clip(0.3 * jax.random.normal(keys[2], (4, N1), jnp.float32), -1.5, 1.5)
    factors = jnp.clip(jax.random.normal(keys[3], (4, NV, N2, N3), jnp.float32), -4.0, 4.0)
    total = scales * noise
    total = total + factors[0][..., None] * loads[0]
    total = total + factors[1][..., None] * loads[1]
    total = total + factors[2][..., None] * loads[2]
    total = total + factors[3][..., None] * loads[3]
    return total.astype(jnp.float32)


def centred(own_key, extent, deviation, limit, held_as=jnp.bfloat16):
    return jnp.clip(deviation * jax.random.normal(own_key, extent, jnp.float32), -limit, limit).astype(held_as)


def setup_inputs(seed: int = 0) -> dict:
    key_list = jax.random.split(jax.random.key(seed), 3)
    return {
        "fields": draw_fields(jax.random.fold_in(key_list[2], 71), 0),
        "start_basis": centred(key_list[1], (N1, RANK), 1.0, 6.0, jnp.float32),
    }


def gram_of(unfolded, count):
    product = lax.dot_general(unfolded.astype(jnp.float32), unfolded.astype(jnp.float32), (((0,), (0,)), ((), ())), precision=lax.Precision.HIGHEST, preferred_element_type=jnp.float32)
    return product / count

def orthonormal(block):
    square = jnp.dot(block.T.astype(jnp.float32), block.astype(jnp.float32), precision=lax.Precision.HIGHEST, preferred_element_type=jnp.float32)
    triangle = jnp.linalg.cholesky(square)
    return lax.linalg.triangular_solve(triangle, block, left_side=False, lower=True, transpose_a=True)

def reference(fields, start_basis):
    unfolded = fields.reshape(-1, N1)
    gram = gram_of(unfolded, float(NV * N2 * N3))
    basis = start_basis
    for sweep in range(SWEEPS):
        block = jnp.dot(gram.astype(jnp.float32), basis.astype(jnp.float32), precision=lax.Precision.HIGHEST, preferred_element_type=jnp.float32)
        basis = orthonormal(block)
    projected = jnp.dot(unfolded.astype(jnp.float32), basis.astype(jnp.float32), precision=lax.Precision.HIGHEST, preferred_element_type=jnp.float32)
    return projected.reshape(NV, N2, N3, RANK)
```

```python
import functools

import jax
import jax.numpy as jnp
from jax import lax
from jax.experimental import pallas as pl
from jax.experimental.pallas import tpu as pltpu
from jax.sharding import PartitionSpec as P

SWEEPS = 4
AXES = ("wide", "slab")
MIB = 1 << 20
HIGHEST = lax.Precision.HIGHEST
NN = (((1,), (0,)), ((), ()))
NT = (((1,), (1,)), ((), ()))
TN = (((0,), (0,)), ((), ()))


def dot(a, b, dims, precision=None):
    return lax.dot_general(a, b, dims, precision=precision, preferred_element_type=jnp.float32)


def halves(x):
    high = x.astype(jnp.bfloat16)
    return high, (x - high.astype(jnp.float32)).astype(jnp.bfloat16)


def exchange(value, axes, mask):
    size = 1
    for axis in axes if isinstance(axes, tuple) else (axes,):
        size *= lax.axis_size(axis)
    return lax.ppermute(value, axes, [(i, i ^ mask) for i in range(size)])


def upper_blocks(blocks):
    return [(i, j) for i in range(blocks) for j in range(i, blocks)]


def gram_kernel(scale, place_ref, x_ref, keep_ref, give_ref, acc, whole):
    step = pl.program_id(0)
    n = x_ref.shape[1]
    half = n // 2
    high, low = halves(x_ref[...])
    left = dot(high[:, :half], jnp.concatenate([high, low], axis=1), TN)
    right = dot(high[:, half:], jnp.concatenate([high[:, half:], low], axis=1), TN)

    @pl.when(step == 0)
    def _():
        acc[:half, :] = left
        acc[half:, half:] = right

    @pl.when(step > 0)
    def _():
        acc[:half, :] += left
        acc[half:, half:] += right

    @pl.when(step == pl.num_programs(0) - 1)
    def _():
        edge = 128
        for number, (i, j) in enumerate(upper_blocks(n // edge)):
            rows, columns = slice(i * edge, (i + 1) * edge), slice(j * edge, (j + 1) * edge)
            cross = acc[rows, n + j * edge : n + (j + 1) * edge]
            other = acc[columns, n + i * edge : n + (i + 1) * edge]
            whole[number * edge : (number + 1) * edge, :] = (
                acc[rows, columns] + cross + other.T
            ) * scale
        place = place_ref[0]
        part = keep_ref.shape[0] // 4
        for k in range(4):
            quarter = ((place >> 1) & 3) ^ k
            mine = pl.multiple_of(((place & 1) * 4 + quarter) * part, 8)
            theirs = pl.multiple_of(((1 - (place & 1)) * 4 + quarter) * part, 8)
            keep_ref[k * part : (k + 1) * part, :] = whole[pl.ds(mine, part), :]
            give_ref[k * part : (k + 1) * part, :] = whole[pl.ds(theirs, part), :]


def local_gram(place, rows, count):
    n = rows.shape[1]
    tile = 512
    tall = len(upper_blocks(n // 128)) * 128
    shape = jax.ShapeDtypeStruct((tall // 2, 128), jnp.float32)
    return pl.pallas_call(
        functools.partial(gram_kernel, 1.0 / count),
        grid=(rows.shape[0] // tile,),
        in_specs=[
            pl.BlockSpec(memory_space=pltpu.SMEM),
            pl.BlockSpec((tile, n), lambda i: (i, 0)),
        ],
        out_specs=[pl.BlockSpec((tall // 2, 128), lambda i: (0, 0))] * 2,
        out_shape=[shape, shape],
        scratch_shapes=[
            pltpu.VMEM((n, 2 * n), jnp.float32),
            pltpu.VMEM((tall, 128), jnp.float32),
        ],
        compiler_params=pltpu.CompilerParams(vmem_limit_bytes=32 * MIB),
        name="local_gram",
    )(place, rows)


def sum_gram(keep, give):
    size = lax.axis_size("wide") * lax.axis_size("slab")
    held = keep + exchange(give, AXES, 1)
    part = held.shape[0] // 4
    pieces = [held[k * part : (k + 1) * part] for k in range(4)]
    total = pieces[0]
    arrived = [exchange(pieces[k], AXES, 2 * k) for k in range(1, 4)]
    for piece in arrived:
        total = total + piece
    mask = 8
    while mask < size:
        total = total + exchange(total, AXES, mask)
        mask *= 2
    mine = jnp.concatenate([total] + [exchange(total, AXES, 2 * k) for k in range(1, 4)])
    return mine, exchange(mine, AXES, 1)


def row_of(x, p):
    return jnp.broadcast_to(x[p : p + 1, :], x.shape)


def column_of(x, k):
    return jnp.broadcast_to(x[:, k : k + 1], x.shape)


def invert_factor(work, result):
    n = work.shape[0]
    lane = lax.broadcasted_iota(jnp.int32, (8, n), 1)
    sub = lax.broadcasted_iota(jnp.int32, (8, n), 0)
    for lo in range(0, n, 8):
        hi = lo + 8
        rows = work[lo:hi, :]
        columns = [column_of(rows, lo + k) for k in range(8)]
        rows = jnp.where((lane >= lo) & (lane < hi), (lane - lo == sub).astype(jnp.float32), rows)
        scaled = jnp.zeros((8, n), jnp.float32)
        for p in range(8):
            pivot = row_of(columns[p], p)
            inverse = 1.0 / pivot
            row = row_of(rows, p)
            here = sub == p
            scaled = jnp.where(here, row * lax.rsqrt(pivot), scaled)
            row = row * inverse
            rows = jnp.where(here, row, rows - columns[p] * row)
            for k in range(p + 1, 8):
                entry = row_of(columns[k], p) * inverse
                columns[k] = jnp.where(here, entry, columns[k] - columns[p] * entry)
        result[lo:hi, :] = jnp.where(lane <= sub + lo, scaled, 0.0)
        if hi < n:
            rest = work[hi:, :]
            lane_rest = lax.broadcasted_iota(jnp.int32, rest.shape, 1)
            update = jnp.where((lane_rest >= lo) & (lane_rest < hi), 0.0, rest)
            for k in range(8):
                update = update - column_of(rest, lo + k) * jnp.broadcast_to(
                    rows[k : k + 1, :], rest.shape
                )
            work[hi:, :] = update


def sweep_kernel(sweeps, place_ref, mine_ref, other_ref, start_ref, block_ref, blocks, gram, work, factor):
    place = place_ref[0]
    part = mine_ref.shape[0] // 4
    for k in range(4):
        quarter = ((place >> 1) & 3) ^ k
        mine = pl.multiple_of(((place & 1) * 4 + quarter) * part, 8)
        theirs = pl.multiple_of(((1 - (place & 1)) * 4 + quarter) * part, 8)
        blocks[pl.ds(mine, part), :] = mine_ref[k * part : (k + 1) * part, :]
        blocks[pl.ds(theirs, part), :] = other_ref[k * part : (k + 1) * part, :]
    edge = 128
    for number, (i, j) in enumerate(upper_blocks(gram.shape[0] // edge)):
        block = blocks[number * edge : (number + 1) * edge, :]
        gram[i * edge : (i + 1) * edge, j * edge : (j + 1) * edge] = block
        if i != j:
            gram[j * edge : (j + 1) * edge, i * edge : (i + 1) * edge] = block.T

    block_ref[...] = dot(start_ref[...].T, gram[...], NN, HIGHEST)

    def sweep(_, carry):
        block = block_ref[...]
        work[...] = dot(block, block, NT, HIGHEST)
        invert_factor(work, factor)
        basis = dot(factor[...], block, NN, HIGHEST)
        block_ref[...] = dot(basis, gram[...], NN, HIGHEST)
        return carry

    lax.fori_loop(0, sweeps - 1, sweep, 0)


def iterate(place, mine, other, start):
    n, rank = start.shape
    vmem = pl.BlockSpec(memory_space=pltpu.VMEM)
    return pl.pallas_call(
        functools.partial(sweep_kernel, SWEEPS),
        in_specs=[pl.BlockSpec(memory_space=pltpu.SMEM), vmem, vmem, vmem],
        out_specs=vmem,
        out_shape=jax.ShapeDtypeStruct((rank, n), jnp.float32),
        scratch_shapes=[
            pltpu.VMEM((2 * mine.shape[0], 128), jnp.float32),
            pltpu.VMEM((n, n), jnp.float32),
            pltpu.VMEM((rank, rank), jnp.float32),
            pltpu.VMEM((rank, rank), jnp.float32),
        ],
        compiler_params=pltpu.CompilerParams(vmem_limit_bytes=32 * MIB),
        name="iterate",
    )(place, mine, other, start)


def factor_kernel(block_ref, out_ref, work):
    block = block_ref[...]
    work[...] = dot(block, block, NT, HIGHEST)
    invert_factor(work, out_ref)


def last_factor(block):
    rank = block.shape[0]
    vmem = pl.BlockSpec(memory_space=pltpu.VMEM)
    return pl.pallas_call(
        factor_kernel,
        in_specs=[vmem],
        out_specs=vmem,
        out_shape=jax.ShapeDtypeStruct((rank, rank), jnp.float32),
        scratch_shapes=[pltpu.VMEM((rank, rank), jnp.float32)],
        compiler_params=pltpu.CompilerParams(vmem_limit_bytes=32 * MIB),
        name="last_factor",
    )(block)


def project_kernel(place_ref, x_ref, block_ref, *refs):
    outs, product = refs[:-1], refs[-1]
    per = 8 // len(outs)
    high, low = halves(x_ref[...])
    block_high, block_low = halves(block_ref[...])
    product[...] = (
        dot(high, block_high, NT) + dot(low, block_high, NT) + dot(high, block_low, NT)
    )
    fibres = x_ref.shape[0] // 8
    for k, out in enumerate(outs):
        to = place_ref[1] ^ k
        for j in range(per):
            out[pl.ds(j, fibres, stride=per), :] = product[pl.ds(to * per + j, fibres, stride=8), :]


def project(place, rows, block, slabs):
    n, rank = rows.shape[1], block.shape[0]
    tile = 512
    size = rows.shape[0] // slabs
    return pl.pallas_call(
        project_kernel,
        grid=(rows.shape[0] // tile,),
        in_specs=[
            pl.BlockSpec(memory_space=pltpu.SMEM),
            pl.BlockSpec((tile, n), lambda i: (i, 0)),
            pl.BlockSpec((rank, n), lambda i: (0, 0)),
        ],
        out_specs=[pl.BlockSpec((tile // slabs, rank), lambda i: (i, 0))] * slabs,
        out_shape=[jax.ShapeDtypeStruct((size, rank), jnp.float32)] * slabs,
        scratch_shapes=[pltpu.VMEM((tile, rank), jnp.float32)],
        compiler_params=pltpu.CompilerParams(vmem_limit_bytes=32 * MIB),
        name="project",
    )(place, rows, block)


def finish_kernel(place_ref, factor_ref, *refs):
    pieces, out = refs[:-1], refs[-1]
    factor = factor_ref[...]
    for k, piece in enumerate(pieces):
        out[0, place_ref[1] ^ k] = dot(piece[0], factor, NT, HIGHEST)


def finish(place, factor, pieces):
    slabs = len(pieces)
    nv, size, rank = pieces[0].shape
    return pl.pallas_call(
        finish_kernel,
        grid=(nv,),
        in_specs=[
            pl.BlockSpec(memory_space=pltpu.SMEM),
            pl.BlockSpec((rank, rank), lambda i: (0, 0)),
        ]
        + [pl.BlockSpec((1, size, rank), lambda i: (i, 0, 0))] * slabs,
        out_specs=pl.BlockSpec((1, slabs, size, rank), lambda i: (i, 0, 0, 0)),
        out_shape=jax.ShapeDtypeStruct((nv, slabs, size, rank), jnp.float32),
        compiler_params=pltpu.CompilerParams(vmem_limit_bytes=32 * MIB),
        name="finish",
    )(place, factor, *pieces)


def per_device(fields, start_basis):
    nv, n2, n3, n1 = fields.shape
    slabs = lax.axis_size("slab")
    slab = lax.axis_index("slab")
    place = jnp.stack([lax.axis_index("wide") * slabs + slab, slab]).astype(jnp.int32)
    rows = fields.reshape(-1, n1)
    count = float(rows.shape[0] * lax.axis_size("wide") * slabs)
    mine, other = sum_gram(*local_gram(place, rows, count))
    block = iterate(place, mine, other, start_basis)
    pieces = project(place, rows, block, slabs)
    pieces = [pieces[0]] + [exchange(pieces[k], "slab", k) for k in range(1, slabs)]
    factor = last_factor(block)
    out = finish(place, factor, [piece.reshape(nv, -1, piece.shape[1]) for piece in pieces])
    return out.reshape(nv, n2 * slabs, n3 // slabs, out.shape[-1])


def solution(mesh):
    in_specs = (P(None, "slab", "wide", None), P())
    out_specs = P(None, None, ("wide", "slab"), None)
    return jax.shard_map(
        per_device, mesh=mesh, in_specs=in_specs, out_specs=out_specs, check_vma=False
    )
```

```python
import functools

import jax
import jax.numpy as jnp
from jax import lax
from jax.experimental import pallas as pl
from jax.experimental.pallas import tpu as pltpu
from jax.sharding import PartitionSpec as P

SWEEPS = 4
SLABS = 4
CHUNKS = 8
EARLY = (1, 2)
TILES = (1, 1, 2, 2, 2)
AXES = ("wide", "slab")
MIB = 1 << 20
HIGHEST = lax.Precision.HIGHEST
NN = (((1,), (0,)), ((), ()))
NT = (((1,), (1,)), ((), ()))
TN = (((0,), (0,)), ((), ()))
BRIEF = pl.CostEstimate(flops=1, bytes_accessed=1, transcendentals=0)


def dot(a, b, dims, precision=None):
    return lax.dot_general(a, b, dims, precision=precision, preferred_element_type=jnp.float32)


def halves(x):
    high = x.astype(jnp.bfloat16)
    return high, (x - high.astype(jnp.float32)).astype(jnp.bfloat16)


def exchange(value, axes, mask):
    size = 1
    for axis in axes if isinstance(axes, tuple) else (axes,):
        size *= lax.axis_size(axis)
    return lax.ppermute(value, axes, [(i, i ^ mask) for i in range(size)])


def upper_blocks(blocks):
    return [(i, j) for i in range(blocks) for j in range(i, blocks)]


def copies(x_ref, held, sems):
    tile = held.shape[1] // sems.shape[0]
    return [
        [
            pltpu.make_async_copy(
                x_ref.at[pl.ds(i * tile, tile), pl.ds(c * 128, 128)],
                held.at[c, pl.ds(i * tile, tile)],
                sems.at[i, c],
            )
            for c in range(held.shape[0])
        ]
        for i in range(sems.shape[0])
    ]


def side_by_side(ref, span):
    return jnp.concatenate([ref[c, span, :] for c in range(ref.shape[0])], axis=1)


def gram_kernel(scale, place_ref, x_ref, *refs):
    keep_ref, give_ref, held = refs[:3]
    early_refs = refs[3:-3]
    acc, whole, sems = refs[-3:]
    n = held.shape[0] * held.shape[2]
    half = n // 2
    arrivals = copies(x_ref, held, sems)
    for arrival in arrivals:
        for copy in arrival:
            copy.start()
    tile = held.shape[1] // len(arrivals)
    first = 0
    for count in TILES:
        for arrival in arrivals[first : first + count]:
            for copy in arrival:
                copy.wait()
        high, low = halves(side_by_side(held, pl.ds(first * tile, count * tile)))
        left = dot(high[:, :half], jnp.concatenate([high, low], axis=1), TN)
        right = dot(high[:, half:], jnp.concatenate([high[:, half:], low], axis=1), TN)
        if first == 0:
            acc[:half, :] = left
            acc[half:, half:] = right
        else:
            acc[:half, :] += left
            acc[half:, half:] += right
        first += count

    per = 8 // SLABS
    begin = 0
    for number, out in enumerate(early_refs):
        to = place_ref[1] ^ (number % 2 + 2)
        fibres = out.shape[1] // per
        for c in range(out.shape[0]):
            for j in range(per):
                out[c, pl.ds(j, fibres, stride=per), :] = held[
                    c, pl.ds(begin + to * per + j, fibres, stride=8), :
                ]
        begin += number % 2 * fibres * 8

    edge = 128
    for number, (i, j) in enumerate(upper_blocks(n // edge)):
        rows, columns = slice(i * edge, (i + 1) * edge), slice(j * edge, (j + 1) * edge)
        cross = acc[rows, n + j * edge : n + (j + 1) * edge]
        other = acc[columns, n + i * edge : n + (i + 1) * edge]
        whole[number * edge : (number + 1) * edge, :] = (
            acc[rows, columns] + cross + other.T
        ) * scale
    place = place_ref[0]
    part = keep_ref.shape[0] // 4
    for k in range(4):
        quarter = ((place >> 2) & 3) ^ k
        mine = pl.multiple_of(((place & 1) * 4 + quarter) * part, 8)
        theirs = pl.multiple_of(((1 - (place & 1)) * 4 + quarter) * part, 8)
        keep_ref[k * part : (k + 1) * part, :] = whole[pl.ds(mine, part), :]
        give_ref[k * part : (k + 1) * part, :] = whole[pl.ds(theirs, part), :]


def local_gram(place, rows, count, early):
    n = rows.shape[1]
    tall = len(upper_blocks(n // 128)) * 128
    half = jax.ShapeDtypeStruct((tall // 2, 128), jnp.float32)
    held = jax.ShapeDtypeStruct((n // 128, rows.shape[0], 128), jnp.float32)
    sent = [
        jax.ShapeDtypeStruct((n // 128, size // SLABS, 128), jnp.float32)
        for size in early
        for _ in range(2)
    ]
    vmem = pl.BlockSpec(memory_space=pltpu.VMEM)
    return pl.pallas_call(
        functools.partial(gram_kernel, 1.0 / count),
        in_specs=[pl.BlockSpec(memory_space=pltpu.SMEM), pl.BlockSpec(memory_space=pl.ANY)],
        out_specs=[vmem] * (3 + len(sent)),
        out_shape=[half, half, held, *sent],
        scratch_shapes=[
            pltpu.VMEM((n, 2 * n), jnp.float32),
            pltpu.VMEM((tall, 128), jnp.float32),
            pltpu.SemaphoreType.DMA((sum(TILES), n // 128)),
        ],
        cost_estimate=BRIEF,
        compiler_params=pltpu.CompilerParams(vmem_limit_bytes=40 * MIB),
        name="local_gram",
    )(place, rows)


def sum_gram(keep, give, send_back):
    size = lax.axis_size("wide") * lax.axis_size("slab")
    held = keep + exchange(give, AXES, 1)
    part = held.shape[0] // 4
    pieces = [held[k * part : (k + 1) * part] for k in range(4)]
    total = pieces[0]
    arrived = [exchange(pieces[k], AXES, 4 * k) for k in range(1, 4)]
    for piece in arrived:
        total = total + piece
    total = total + exchange(total, AXES, 2)
    total, extra = send_back(total)
    mask = 16
    while mask < size:
        total = total + exchange(total, AXES, mask)
        mask *= 2
    mine = jnp.concatenate([total] + [exchange(total, AXES, 4 * k) for k in range(1, 4)])
    mine, extra = lax.optimization_barrier((mine, extra))
    return mine, exchange(mine, AXES, 1), extra


def row_of(x, p):
    return jnp.broadcast_to(x[p : p + 1, :], x.shape)


def column_of(x, k):
    return jnp.broadcast_to(x[:, k : k + 1], x.shape)


def invert_factor(work, result):
    n = work.shape[0]
    lane = lax.broadcasted_iota(jnp.int32, (8, n), 1)
    sub = lax.broadcasted_iota(jnp.int32, (8, n), 0)
    for lo in range(0, n, 8):
        hi = lo + 8
        rows = work[lo:hi, :]
        columns = [column_of(rows, lo + k) for k in range(8)]
        rows = jnp.where((lane >= lo) & (lane < hi), (lane - lo == sub).astype(jnp.float32), rows)
        scaled = jnp.zeros((8, n), jnp.float32)
        for p in range(8):
            pivot = row_of(columns[p], p)
            inverse = 1.0 / pivot
            row = row_of(rows, p)
            here = sub == p
            scaled = jnp.where(here, row * lax.rsqrt(pivot), scaled)
            row = row * inverse
            rows = jnp.where(here, row, rows - columns[p] * row)
            for k in range(p + 1, 8):
                entry = row_of(columns[k], p) * inverse
                columns[k] = jnp.where(here, entry, columns[k] - columns[p] * entry)
        result[lo:hi, :] = jnp.where(lane <= sub + lo, scaled, 0.0)
        if hi < n:
            rest = work[hi:, :]
            lane_rest = lax.broadcasted_iota(jnp.int32, rest.shape, 1)
            update = jnp.where((lane_rest >= lo) & (lane_rest < hi), 0.0, rest)
            for k in range(8):
                update = update - column_of(rest, lo + k) * jnp.broadcast_to(
                    rows[k : k + 1, :], rest.shape
                )
            work[hi:, :] = update


def sweep_kernel(sweeps, place_ref, mine_ref, other_ref, start_ref, block_ref, blocks, gram, work, factor):
    place = place_ref[0]
    part = mine_ref.shape[0] // 4
    for k in range(4):
        quarter = ((place >> 2) & 3) ^ k
        mine = pl.multiple_of(((place & 1) * 4 + quarter) * part, 8)
        theirs = pl.multiple_of(((1 - (place & 1)) * 4 + quarter) * part, 8)
        blocks[pl.ds(mine, part), :] = mine_ref[k * part : (k + 1) * part, :]
        blocks[pl.ds(theirs, part), :] = other_ref[k * part : (k + 1) * part, :]
    edge = 128
    for number, (i, j) in enumerate(upper_blocks(gram.shape[0] // edge)):
        block = blocks[number * edge : (number + 1) * edge, :]
        gram[i * edge : (i + 1) * edge, j * edge : (j + 1) * edge] = block
        if i != j:
            gram[j * edge : (j + 1) * edge, i * edge : (i + 1) * edge] = block.T

    block_ref[...] = dot(start_ref[...].T, gram[...], NN, HIGHEST)

    def sweep(_, carry):
        block = block_ref[...]
        work[...] = dot(block, block, NT, HIGHEST)
        invert_factor(work, factor)
        basis = dot(factor[...], block, NN, HIGHEST)
        block_ref[...] = dot(basis, gram[...], NN, HIGHEST)
        return carry

    lax.fori_loop(0, sweeps - 1, sweep, 0)


def iterate(place, mine, other, start):
    n, rank = start.shape
    vmem = pl.BlockSpec(memory_space=pltpu.VMEM)
    return pl.pallas_call(
        functools.partial(sweep_kernel, SWEEPS),
        in_specs=[pl.BlockSpec(memory_space=pltpu.SMEM), vmem, vmem, vmem],
        out_specs=vmem,
        out_shape=jax.ShapeDtypeStruct((rank, n), jnp.float32),
        scratch_shapes=[
            pltpu.VMEM((2 * mine.shape[0], 128), jnp.float32),
            pltpu.VMEM((n, n), jnp.float32),
            pltpu.VMEM((rank, rank), jnp.float32),
            pltpu.VMEM((rank, rank), jnp.float32),
        ],
        cost_estimate=BRIEF,
        compiler_params=pltpu.CompilerParams(vmem_limit_bytes=16 * MIB),
        name="iterate",
    )(place, mine, other, start)


def factor_kernel(block_ref, out_ref, work):
    block = block_ref[...]
    work[...] = dot(block, block, NT, HIGHEST)
    invert_factor(work, out_ref)


def last_factor(block):
    rank = block.shape[0]
    vmem = pl.BlockSpec(memory_space=pltpu.VMEM)
    return pl.pallas_call(
        factor_kernel,
        in_specs=[vmem],
        out_specs=vmem,
        out_shape=jax.ShapeDtypeStruct((rank, rank), jnp.float32),
        scratch_shapes=[pltpu.VMEM((rank, rank), jnp.float32)],
        cost_estimate=BRIEF,
        compiler_params=pltpu.CompilerParams(vmem_limit_bytes=16 * MIB),
        name="last_factor",
    )(block)


def weights(block_ref):
    return jnp.concatenate(halves(block_ref[...]), axis=0)


def halved_product(x, both):
    high, low = halves(x)
    rank = both.shape[0] // 2
    product = dot(high, both, NT)
    return product[:, :rank] + product[:, rank:] + dot(low, both[:rank], NT)


def project_kernel(ranks, begins, place_ref, held, block_ref, *outs):
    per = 8 // SLABS
    both = weights(block_ref)
    for begin in sorted(set(begins)):
        some = [(k, out) for k, b, out in zip(ranks, begins, outs, strict=True) if b == begin]
        total = some[0][1].shape[0] // per
        fibres = total // pl.cdiv(total * len(some), 512)
        for first in range(0, total, fibres):
            picks = [
                pl.ds(begin + first * 8 + (place_ref[1] ^ k) * per + j, fibres, stride=8)
                for k, _ in some
                for j in range(per)
            ]
            x = jnp.concatenate([side_by_side(held, pick) for pick in picks], axis=0)
            product = halved_product(x, both)
            for number in range(len(picks)):
                out = some[number // per][1]
                place = pl.ds(first * per + number % per, fibres, stride=per)
                out[place, :] = product[number * fibres : (number + 1) * fibres]


def project(place, held, block, ranks, begins, name):
    rows, rank = held.shape[1], block.shape[0]
    vmem = pl.BlockSpec(memory_space=pltpu.VMEM)
    return pl.pallas_call(
        functools.partial(project_kernel, ranks, begins),
        in_specs=[pl.BlockSpec(memory_space=pltpu.SMEM), vmem, vmem],
        out_specs=[vmem] * len(ranks),
        out_shape=[
            jax.ShapeDtypeStruct(((rows - begin) // SLABS, rank), jnp.float32) for begin in begins
        ],
        cost_estimate=BRIEF,
        compiler_params=pltpu.CompilerParams(vmem_limit_bytes=16 * MIB),
        name=name,
    )(place, held, block)


def arrived_kernel(block_ref, *refs):
    outs = refs[-2:]
    each = (len(refs) - 2) // 2
    both = weights(block_ref)
    for k, out in enumerate(outs):
        begin = 0
        for x_ref in refs[k * each : (k + 1) * each]:
            size = x_ref.shape[1]
            x = side_by_side(x_ref, slice(None))
            out[begin : begin + size, :] = halved_product(x, both)
            begin += size


def project_arrived(block, arrived):
    vmem = pl.BlockSpec(memory_space=pltpu.VMEM)
    rows = sum(x.shape[1] for x in arrived) // 2
    return pl.pallas_call(
        arrived_kernel,
        in_specs=[vmem] * (1 + len(arrived)),
        out_specs=[vmem] * 2,
        out_shape=[jax.ShapeDtypeStruct((rows, block.shape[0]), jnp.float32)] * 2,
        cost_estimate=BRIEF,
        compiler_params=pltpu.CompilerParams(vmem_limit_bytes=16 * MIB),
        name="project_arrived",
    )(block, *arrived)


def finish_kernel(pair, first, place_ref, factor_ref, *refs):
    pieces = refs[:2]
    out, results, sems = refs[-3:]
    factor = factor_ref[...]
    per, size = out.shape[2], out.shape[3]
    count = results.shape[1]
    runs = []
    while sum(length for _, length in runs) < count:
        begin = first + sum(length for _, length in runs)
        runs.append((begin, min(per - begin % per, first + count - begin)))
    sends = []
    for k, piece in enumerate(pieces):
        results[k] = dot(piece[...], factor, NT, HIGHEST).reshape(results.shape[1:])
        for number, (begin, length) in enumerate(runs):
            send = pltpu.make_async_copy(
                results.at[k, pl.ds(begin - first, length)],
                out.at[begin // per, place_ref[1] ^ (2 * pair + k), pl.ds(begin % per, length)],
                sems.at[k, number],
            )
            send.start()
            sends.append(send)
    for send in sends:
        send.wait()


def finish(place, factor, pieces, pair, first, into, name):
    shape = into if isinstance(into, tuple) else into.shape
    size, rank = shape[3:]
    count = pieces[0].shape[0] // size
    vmem = pl.BlockSpec(memory_space=pltpu.VMEM)
    in_specs = [pl.BlockSpec(memory_space=pltpu.SMEM)] + [vmem] * 3
    operands = [place, factor, *pieces]
    aliases = {}
    if not isinstance(into, tuple):
        aliases = {len(operands): 0}
        in_specs.append(pl.BlockSpec(memory_space=pl.ANY))
        operands.append(into)
    return pl.pallas_call(
        functools.partial(finish_kernel, pair, first),
        in_specs=in_specs,
        out_specs=pl.BlockSpec(memory_space=pl.ANY),
        out_shape=jax.ShapeDtypeStruct(shape, jnp.float32),
        scratch_shapes=[
            pltpu.VMEM((2, count, size, rank), jnp.float32),
            pltpu.SemaphoreType.DMA((2, shape[0])),
        ],
        input_output_aliases=aliases,
        cost_estimate=BRIEF,
        compiler_params=pltpu.CompilerParams(vmem_limit_bytes=16 * MIB),
        name=name,
    )(*operands)


def per_device(fields, start_basis):
    nv, n2, n3, n1 = fields.shape
    slabs = lax.axis_size("slab")
    slab = lax.axis_index("slab")
    place = jnp.stack([lax.axis_index("wide") * slabs + slab, slab]).astype(jnp.int32)
    rows = fields.reshape(-1, n1)
    count = float(rows.shape[0] * lax.axis_size("wide") * slabs)
    early = [some * rows.shape[0] // CHUNKS for some in EARLY]

    keep, give, held, *sent = local_gram(place, rows, count, early)

    def first_early(total):
        total, *some = lax.optimization_barrier((total, *sent[:2]))
        return total, [exchange(x, "slab", 2 + k) for k, x in enumerate(some)]

    mine, other, arrived = sum_gram(keep, give, first_early)
    more, arrived = lax.optimization_barrier((sent[2:], arrived))
    more = [exchange(x, "slab", 2 + k) for k, x in enumerate(more)]
    arrived = [x for pair in zip(arrived, more, strict=True) for x in pair]
    block = iterate(place, mine, other, start_basis)

    late = sum(early)
    near, *far = project(place, held, block, (1, 2, 3), (0, late, late), "project_sent")
    block, near, *far = lax.optimization_barrier((block, near, *far))
    far = [exchange(x, "slab", 2 + k) for k, x in enumerate(far)]
    near = [*project(place, held, block, (0,), (0,), "project_own"), exchange(near, "slab", 1)]
    arrived = project_arrived(block, arrived)
    factor = last_factor(block)

    per = CHUNKS // nv
    out = (nv, slabs, per, n2 * n3 // slabs // per, block.shape[0])
    out = finish(place, factor, near, 0, 0, out, "finish_near")
    out = finish(place, factor, arrived, 1, 0, out, "finish_arrived")
    out = finish(place, factor, far, 1, sum(EARLY), out, "finish_far")
    return out.reshape(nv, n2 * slabs, n3 // slabs, out.shape[-1])


def solution(mesh):
    in_specs = (P(None, "slab", "wide", None), P())
    out_specs = P(None, None, ("wide", "slab"), None)
    return jax.shard_map(
        per_device, mesh=mesh, in_specs=in_specs, out_specs=out_specs, check_vma=False
    )
```

```python
import functools

import jax
import jax.numpy as jnp
from jax import lax
from jax.experimental import pallas as pl
from jax.experimental.pallas import tpu as pltpu
from jax.sharding import PartitionSpec as P

SWEEPS = 4
SLABS = 4
CHUNKS = 16
EARLY = 4
TILES = (1, 1, 2, 2, 2)
AXES = ("wide", "slab")
MIB = 1 << 20
HIGHEST = lax.Precision.HIGHEST
NN = (((1,), (0,)), ((), ()))
NT = (((1,), (1,)), ((), ()))
TN = (((0,), (0,)), ((), ()))
BRIEF = pl.CostEstimate(flops=1, bytes_accessed=1, transcendentals=0)


def dot(a, b, dims, precision=None):
    return lax.dot_general(a, b, dims, precision=precision, preferred_element_type=jnp.float32)


def halves(x):
    high = x.astype(jnp.bfloat16)
    return high, (x - high.astype(jnp.float32)).astype(jnp.bfloat16)


def exchange(value, axes, mask):
    size = 1
    for axis in axes if isinstance(axes, tuple) else (axes,):
        size *= lax.axis_size(axis)
    return lax.ppermute(value, axes, [(i, i ^ mask) for i in range(size)])


def upper_blocks(blocks):
    return [(i, j) for i in range(blocks) for j in range(i, blocks)]


def copies(x_ref, held, sems):
    tile = held.shape[1] // sems.shape[0]
    return [
        [
            pltpu.make_async_copy(
                x_ref.at[pl.ds(i * tile, tile), pl.ds(c * 128, 128)],
                held.at[c, pl.ds(i * tile, tile)],
                sems.at[i, c],
            )
            for c in range(held.shape[0])
        ]
        for i in range(sems.shape[0])
    ]


def side_by_side(ref, span):
    return jnp.concatenate([ref[c, span, :] for c in range(ref.shape[0])], axis=1)


def gram_kernel(scale, place_ref, x_ref, *refs):
    keep_ref, give_ref, held = refs[:3]
    early_refs = refs[3:-3]
    acc, whole, sems = refs[-3:]
    n = held.shape[0] * held.shape[2]
    half = n // 2
    arrivals = copies(x_ref, held, sems)
    for arrival in arrivals:
        for copy in arrival:
            copy.start()
    tile = held.shape[1] // len(arrivals)
    first = 0
    for count in TILES:
        for arrival in arrivals[first : first + count]:
            for copy in arrival:
                copy.wait()
        high, low = halves(side_by_side(held, pl.ds(first * tile, count * tile)))
        left = dot(high[:, :half], jnp.concatenate([high, low], axis=1), TN)
        right = dot(high[:, half:], jnp.concatenate([high[:, half:], low], axis=1), TN)
        if first == 0:
            acc[:half, :] = left
            acc[half:, half:] = right
        else:
            acc[:half, :] += left
            acc[half:, half:] += right
        first += count

    per = 8 // SLABS
    for number, out in enumerate(early_refs):
        to = place_ref[1] ^ (number + 2)
        fibres = out.shape[1] // per
        for c in range(out.shape[0]):
            for j in range(per):
                out[c, pl.ds(j, fibres, stride=per), :] = held[
                    c, pl.ds(to * per + j, fibres, stride=8), :
                ]

    edge = 128
    for number, (i, j) in enumerate(upper_blocks(n // edge)):
        rows, columns = slice(i * edge, (i + 1) * edge), slice(j * edge, (j + 1) * edge)
        cross = acc[rows, n + j * edge : n + (j + 1) * edge]
        other = acc[columns, n + i * edge : n + (i + 1) * edge]
        whole[number * edge : (number + 1) * edge, :] = (
            acc[rows, columns] + cross + other.T
        ) * scale
    place = place_ref[0]
    part = keep_ref.shape[0] // 4
    for k in range(4):
        quarter = ((place >> 2) & 3) ^ k
        mine = pl.multiple_of(((place & 1) * 4 + quarter) * part, 8)
        theirs = pl.multiple_of(((1 - (place & 1)) * 4 + quarter) * part, 8)
        keep_ref[k * part : (k + 1) * part, :] = whole[pl.ds(mine, part), :]
        give_ref[k * part : (k + 1) * part, :] = whole[pl.ds(theirs, part), :]


def local_gram(place, rows, count, early):
    n = rows.shape[1]
    tall = len(upper_blocks(n // 128)) * 128
    half = jax.ShapeDtypeStruct((tall // 2, 128), jnp.float32)
    held = jax.ShapeDtypeStruct((n // 128, rows.shape[0], 128), jnp.float32)
    sent = jax.ShapeDtypeStruct((n // 128, early // SLABS, 128), jnp.float32)
    vmem = pl.BlockSpec(memory_space=pltpu.VMEM)
    return pl.pallas_call(
        functools.partial(gram_kernel, 1.0 / count),
        in_specs=[pl.BlockSpec(memory_space=pltpu.SMEM), pl.BlockSpec(memory_space=pl.ANY)],
        out_specs=[vmem] * 5,
        out_shape=[half, half, held, sent, sent],
        scratch_shapes=[
            pltpu.VMEM((n, 2 * n), jnp.float32),
            pltpu.VMEM((tall, 128), jnp.float32),
            pltpu.SemaphoreType.DMA((sum(TILES), n // 128)),
        ],
        cost_estimate=BRIEF,
        compiler_params=pltpu.CompilerParams(vmem_limit_bytes=40 * MIB),
        name="local_gram",
    )(place, rows)


def sum_gram(keep, give, sent):
    size = lax.axis_size("wide") * lax.axis_size("slab")
    held = keep + exchange(give, AXES, 1)
    part = held.shape[0] // 4
    pieces = [held[k * part : (k + 1) * part] for k in range(4)]
    total = pieces[0]
    arrived = [exchange(pieces[k], AXES, 4 * k) for k in range(1, 4)]
    for piece in arrived:
        total = total + piece
    total = total + exchange(total, AXES, 2)
    total, *sent = lax.optimization_barrier((total, *sent))
    mask = 16
    while mask < size:
        total = total + exchange(total, AXES, mask)
        mask *= 2
    mine = jnp.concatenate([total] + [exchange(total, AXES, 4 * k) for k in range(1, 4)])
    return mine, exchange(mine, AXES, 1), sent


def row_of(x, p):
    return jnp.broadcast_to(x[p : p + 1, :], x.shape)


def column_of(x, k):
    return jnp.broadcast_to(x[:, k : k + 1], x.shape)


def total(terms):
    while len(terms) > 1:
        odd = terms[len(terms) & ~1 :]
        terms = [x + y for x, y in zip(terms[::2], terms[1::2], strict=False)] + odd
    return terms[0]


def invert_factor(work, result):
    n = work.shape[0]
    lane = lax.broadcasted_iota(jnp.int32, (8, n), 1)
    sub = lax.broadcasted_iota(jnp.int32, (8, n), 0)
    columns = [column_of(work[:8, :], k) for k in range(8)]
    for lo in range(0, n, 8):
        hi = lo + 8
        rows = work[lo:hi, :]
        if hi < n:
            rest = work[hi:, :]
            factors = [column_of(rest, lo + k) for k in range(8)]
            across = [column_of(rows, hi + k) for k in range(8)]
            later = [column_of(rest[:8], hi + k) for k in range(8)]
            under = [x[:8] for x in factors]
        rows = jnp.where((lane >= lo) & (lane < hi), (lane - lo == sub).astype(jnp.float32), rows)
        scaled = jnp.zeros((8, n), jnp.float32)
        for p in range(8):
            here = sub == p
            column = columns[p]
            pivot = row_of(column, p)
            inverse = 1.0 / pivot
            row = row_of(rows, p)
            scaled = jnp.where(here, row * lax.rsqrt(pivot), scaled)
            row = row * inverse
            rows = jnp.where(here, row, rows - column * row)
            for k in range(8 if hi < n else 0):
                if k == p:
                    continue
                entry = row_of(columns[k], p)
                if k == p + 1:
                    kept = jnp.where(here, 0.0, columns[k])
                    columns[k] = kept - jnp.where(here, -entry, column * entry) * inverse
                else:
                    columns[k] = jnp.where(here, entry * inverse, columns[k] - column * (entry * inverse))
                under[k] = under[k] - under[p] * (entry * inverse)
            if hi < n:
                columns[p] = jnp.where(here, inverse, -column * inverse)
                under[p] = -under[p] * inverse
            else:
                for k in range(p + 1, 8):
                    entry = row_of(columns[k], p) * inverse
                    columns[k] = jnp.where(here, entry, columns[k] - column * entry)
        result[lo:hi, :] = jnp.where(lane <= sub + lo, scaled, 0.0)
        if hi < n:
            columns = [
                later[k] + total([under[p] * row_of(across[k], p) for p in range(8)])
                for k in range(8)
            ]
            lane_rest = lax.broadcasted_iota(jnp.int32, rest.shape, 1)
            kept = jnp.where((lane_rest >= lo) & (lane_rest < hi), 0.0, rest)
            work[hi:, :] = kept - total(
                [factors[k] * jnp.broadcast_to(rows[k : k + 1, :], rest.shape) for k in range(8)]
            )


def sweep_kernel(
    sweeps, place_ref, mine_ref, other_ref, start_ref, block_ref, blocks, gram, gram_high, gram_low,
    ahead, work, factor,
):
    place = place_ref[0]
    part = mine_ref.shape[0] // 4
    for k in range(4):
        quarter = ((place >> 2) & 3) ^ k
        mine = pl.multiple_of(((place & 1) * 4 + quarter) * part, 8)
        theirs = pl.multiple_of(((1 - (place & 1)) * 4 + quarter) * part, 8)
        blocks[pl.ds(mine, part), :] = mine_ref[k * part : (k + 1) * part, :]
        blocks[pl.ds(theirs, part), :] = other_ref[k * part : (k + 1) * part, :]
    edge = 128
    for number, (i, j) in enumerate(upper_blocks(gram.shape[0] // edge)):
        block = blocks[number * edge : (number + 1) * edge, :]
        gram[i * edge : (i + 1) * edge, j * edge : (j + 1) * edge] = block
        if i != j:
            gram[j * edge : (j + 1) * edge, i * edge : (i + 1) * edge] = block.T

    gram_high[...], gram_low[...] = halves(gram[...])

    def by_gram(block):
        high, low = halves(block)
        both = dot(jnp.concatenate([high, low], axis=0), gram_high[...], NN)
        rank = block.shape[0]
        return both[:rank] + both[rank:] + dot(high, gram_low[...], NN)

    block_ref[...] = by_gram(start_ref[...].T)

    def sweep(_, carry):
        block = block_ref[...]
        work[...] = dot(block, block, NT, HIGHEST)
        ahead[...] = by_gram(block)
        invert_factor(work, factor)
        block_ref[...] = dot(factor[...], ahead[...], NN, HIGHEST)
        return carry

    lax.fori_loop(0, sweeps - 1, sweep, 0)


def iterate(place, mine, other, start):
    n, rank = start.shape
    vmem = pl.BlockSpec(memory_space=pltpu.VMEM)
    return pl.pallas_call(
        functools.partial(sweep_kernel, SWEEPS),
        in_specs=[pl.BlockSpec(memory_space=pltpu.SMEM), vmem, vmem, vmem],
        out_specs=vmem,
        out_shape=jax.ShapeDtypeStruct((rank, n), jnp.float32),
        scratch_shapes=[
            pltpu.VMEM((2 * mine.shape[0], 128), jnp.float32),
            pltpu.VMEM((n, n), jnp.float32),
            pltpu.VMEM((n, n), jnp.bfloat16),
            pltpu.VMEM((n, n), jnp.bfloat16),
            pltpu.VMEM((rank, n), jnp.float32),
            pltpu.VMEM((rank, rank), jnp.float32),
            pltpu.VMEM((rank, rank), jnp.float32),
        ],
        cost_estimate=BRIEF,
        compiler_params=pltpu.CompilerParams(vmem_limit_bytes=16 * MIB),
        name="iterate",
    )(place, mine, other, start)


def factor_kernel(block_ref, out_ref, work):
    block = block_ref[...]
    work[...] = dot(block, block, NT, HIGHEST)
    invert_factor(work, out_ref)


def last_factor(block):
    rank = block.shape[0]
    vmem = pl.BlockSpec(memory_space=pltpu.VMEM)
    return pl.pallas_call(
        factor_kernel,
        in_specs=[vmem],
        out_specs=vmem,
        out_shape=jax.ShapeDtypeStruct((rank, rank), jnp.float32),
        scratch_shapes=[pltpu.VMEM((rank, rank), jnp.float32)],
        cost_estimate=BRIEF,
        compiler_params=pltpu.CompilerParams(vmem_limit_bytes=16 * MIB),
        name="last_factor",
    )(block)


def weights(block_ref):
    return jnp.concatenate(halves(block_ref[...]), axis=0)


def halved_product(x, both):
    high, low = halves(x)
    rank = both.shape[0] // 2
    product = dot(high, both, NT)
    return product[:, :rank] + product[:, rank:] + dot(low, both[:rank], NT)


def project_kernel(ranks, begins, place_ref, held, block_ref, *outs):
    per = 8 // SLABS
    both = weights(block_ref)
    for begin in sorted(set(begins)):
        some = [(k, out) for k, b, out in zip(ranks, begins, outs, strict=True) if b == begin]
        total = some[0][1].shape[0] // per
        fibres = total // pl.cdiv(total * len(some), 512)
        for first in range(0, total, fibres):
            picks = [
                pl.ds(begin + first * 8 + (place_ref[1] ^ k) * per + j, fibres, stride=8)
                for k, _ in some
                for j in range(per)
            ]
            x = jnp.concatenate([side_by_side(held, pick) for pick in picks], axis=0)
            product = halved_product(x, both)
            for number in range(len(picks)):
                out = some[number // per][1]
                place = pl.ds(first * per + number % per, fibres, stride=per)
                out[place, :] = product[number * fibres : (number + 1) * fibres]


def project(place, held, block, ranks, begins, name):
    rows, rank = held.shape[1], block.shape[0]
    vmem = pl.BlockSpec(memory_space=pltpu.VMEM)
    return pl.pallas_call(
        functools.partial(project_kernel, ranks, begins),
        in_specs=[pl.BlockSpec(memory_space=pltpu.SMEM), vmem, vmem],
        out_specs=[vmem] * len(ranks),
        out_shape=[
            jax.ShapeDtypeStruct(((rows - begin) // SLABS, rank), jnp.float32) for begin in begins
        ],
        cost_estimate=BRIEF,
        compiler_params=pltpu.CompilerParams(vmem_limit_bytes=16 * MIB),
        name=name,
    )(place, held, block)


def arrived_kernel(block_ref, *refs):
    both = weights(block_ref)
    half = len(refs) // 2
    for x_ref, out in zip(refs[:half], refs[half:], strict=True):
        out[...] = halved_product(side_by_side(x_ref, slice(None)), both)


def project_arrived(block, arrived):
    vmem = pl.BlockSpec(memory_space=pltpu.VMEM)
    return pl.pallas_call(
        arrived_kernel,
        in_specs=[vmem] * (1 + len(arrived)),
        out_specs=[vmem] * len(arrived),
        out_shape=[jax.ShapeDtypeStruct((x.shape[1], block.shape[0]), jnp.float32) for x in arrived],
        cost_estimate=BRIEF,
        compiler_params=pltpu.CompilerParams(vmem_limit_bytes=16 * MIB),
        name="project_arrived",
    )(block, *arrived)


def finish_kernel(ranks, first, place_ref, factor_ref, *refs):
    pieces = refs[: len(ranks)]
    out, results, sems = refs[-3:]
    factor = factor_ref[...]
    per, size = out.shape[2], out.shape[3]
    count = results.shape[1]
    runs = []
    while sum(length for _, length in runs) < count:
        begin = first + sum(length for _, length in runs)
        runs.append((begin, min(per - begin % per, first + count - begin)))
    sends = []
    for k, (rank, piece) in enumerate(zip(ranks, pieces, strict=True)):
        for number, (begin, length) in enumerate(runs):
            span = pl.ds(begin - first, length)
            rows = piece[(begin - first) * size : (begin - first + length) * size, :]
            results[k, span] = dot(rows, factor, NT, HIGHEST).reshape(length, size, -1)
            send = pltpu.make_async_copy(
                results.at[k, span],
                out.at[begin // per, place_ref[1] ^ rank, pl.ds(begin % per, length)],
                sems.at[k, number],
            )
            send.start()
            sends.append(send)
    for send in sends:
        send.wait()


def finish(place, factor, pieces, ranks, first, into, name):
    shape = into if isinstance(into, tuple) else into.shape
    size, rank = shape[3:]
    count = pieces[0].shape[0] // size
    vmem = pl.BlockSpec(memory_space=pltpu.VMEM)
    in_specs = [pl.BlockSpec(memory_space=pltpu.SMEM)] + [vmem] * (1 + len(pieces))
    operands = [place, factor, *pieces]
    aliases = {}
    if not isinstance(into, tuple):
        aliases = {len(operands): 0}
        in_specs.append(pl.BlockSpec(memory_space=pl.ANY))
        operands.append(into)
    return pl.pallas_call(
        functools.partial(finish_kernel, ranks, first),
        in_specs=in_specs,
        out_specs=pl.BlockSpec(memory_space=pl.ANY),
        out_shape=jax.ShapeDtypeStruct(shape, jnp.float32),
        scratch_shapes=[
            pltpu.VMEM((len(pieces), count, size, rank), jnp.float32),
            pltpu.SemaphoreType.DMA((len(pieces), shape[0])),
        ],
        input_output_aliases=aliases,
        cost_estimate=BRIEF,
        compiler_params=pltpu.CompilerParams(vmem_limit_bytes=16 * MIB),
        name=name,
    )(*operands)


def per_device(fields, start_basis):
    nv, n2, n3, n1 = fields.shape
    slabs = lax.axis_size("slab")
    slab = lax.axis_index("slab")
    place = jnp.stack([lax.axis_index("wide") * slabs + slab, slab]).astype(jnp.int32)
    rows = fields.reshape(-1, n1)
    count = float(rows.shape[0] * lax.axis_size("wide") * slabs)
    early = EARLY * rows.shape[0] // CHUNKS

    def to_far(some):
        return [exchange(x, "slab", 2 + k) for k, x in enumerate(some)]

    keep, give, held, *sent = local_gram(place, rows, count, early)
    mine, other, sent = sum_gram(keep, give, sent)
    arrived = to_far(sent)
    block = iterate(place, mine, other, start_basis)

    block, *arrived = lax.optimization_barrier((block, *arrived))
    near, *far = project(place, held, block, (1, 2, 3), (0, early, early), "project_sent")
    block, near, *far = lax.optimization_barrier((block, near, *far))
    far = to_far(far)
    near = exchange(near, "slab", 1)
    (own,) = project(place, held, block, (0,), (0,), "project_own")
    arrived = project_arrived(block, arrived)
    factor = last_factor(block)

    per = CHUNKS // nv
    out = (nv, slabs, per, n2 * n3 // slabs // per, block.shape[0])
    out = finish(place, factor, arrived, (2, 3), 0, out, "finish_arrived")
    out = finish(place, factor, far[:1], (2,), EARLY, out, "finish_first_far")
    out = finish(place, factor, [own, near], (0, 1), 0, out, "finish_near")
    out = finish(place, factor, far[1:], (3,), EARLY, out, "finish_last_far")
    return out.reshape(nv, n2 * slabs, n3 // slabs, out.shape[-1])


def solution(mesh):
    in_specs = (P(None, "slab", "wide", None), P())
    out_specs = P(None, None, ("wide", "slab"), None)
    return jax.shard_map(
        per_device, mesh=mesh, in_specs=in_specs, out_specs=out_specs, check_vma=False
    )
```

```python
import functools

import jax
import jax.numpy as jnp
from jax import lax
from jax.experimental import pallas as pl
from jax.experimental.pallas import tpu as pltpu
from jax.sharding import PartitionSpec as P

SWEEPS = 4
SLABS = 4
CHUNKS = 16
EARLY = ((3, 0, 2), (2, 0, 3), (3, 2, 3))
FAR = (2, 3)
TILES = (1, 1, 2, 2, 2)
AXES = ("wide", "slab")
MIB = 1 << 20
HIGHEST = lax.Precision.HIGHEST
NN = (((1,), (0,)), ((), ()))
NT = (((1,), (1,)), ((), ()))
TN = (((0,), (0,)), ((), ()))
BRIEF = pl.CostEstimate(flops=1, bytes_accessed=1, transcendentals=0)


def dot(a, b, dims, precision=None):
    return lax.dot_general(a, b, dims, precision=precision, preferred_element_type=jnp.float32)


def halves(x):
    high = x.astype(jnp.bfloat16)
    return high, (x - high.astype(jnp.float32)).astype(jnp.bfloat16)


def exchange(value, axes, mask):
    size = 1
    for axis in axes if isinstance(axes, tuple) else (axes,):
        size *= lax.axis_size(axis)
    return lax.ppermute(value, axes, [(i, i ^ mask) for i in range(size)])


def upper_blocks(blocks):
    return [(i, j) for i in range(blocks) for j in range(i, blocks)]


def copies(x_ref, held, sems):
    tile = held.shape[1] // sems.shape[0]
    return [
        [
            pltpu.make_async_copy(
                x_ref.at[pl.ds(i * tile, tile), pl.ds(c * 128, 128)],
                held.at[c, pl.ds(i * tile, tile)],
                sems.at[i, c],
            )
            for c in range(held.shape[0])
        ]
        for i in range(sems.shape[0])
    ]


def side_by_side(ref, span):
    return jnp.concatenate([ref[c, span, :] for c in range(ref.shape[0])], axis=1)


def gram_kernel(scale, place_ref, x_ref, *refs):
    keep_ref, give_ref, held, acc, whole, sems = refs
    n = held.shape[0] * held.shape[2]
    half = n // 2
    arrivals = copies(x_ref, held, sems)
    for arrival in arrivals:
        for copy in arrival:
            copy.start()
    tile = held.shape[1] // len(arrivals)
    first = 0
    for count in TILES:
        for arrival in arrivals[first : first + count]:
            for copy in arrival:
                copy.wait()
        high, low = halves(side_by_side(held, pl.ds(first * tile, count * tile)))
        left = dot(high[:, :half], jnp.concatenate([high, low], axis=1), TN)
        right = dot(high[:, half:], jnp.concatenate([high[:, half:], low], axis=1), TN)
        if first == 0:
            acc[:half, :] = left
            acc[half:, half:] = right
        else:
            acc[:half, :] += left
            acc[half:, half:] += right
        first += count

    edge = 128
    for number, (i, j) in enumerate(upper_blocks(n // edge)):
        rows, columns = slice(i * edge, (i + 1) * edge), slice(j * edge, (j + 1) * edge)
        cross = acc[rows, n + j * edge : n + (j + 1) * edge]
        other = acc[columns, n + i * edge : n + (i + 1) * edge]
        whole[number * edge : (number + 1) * edge, :] = (
            acc[rows, columns] + cross + other.T
        ) * scale
    place = place_ref[0]
    part = keep_ref.shape[0] // 4
    for k in range(4):
        quarter = ((place >> 2) & 3) ^ k
        mine = pl.multiple_of(((place & 1) * 4 + quarter) * part, 8)
        theirs = pl.multiple_of(((1 - (place & 1)) * 4 + quarter) * part, 8)
        keep_ref[k * part : (k + 1) * part, :] = whole[pl.ds(mine, part), :]
        give_ref[k * part : (k + 1) * part, :] = whole[pl.ds(theirs, part), :]


def local_gram(place, rows, count):
    n = rows.shape[1]
    tall = len(upper_blocks(n // 128)) * 128
    half = jax.ShapeDtypeStruct((tall // 2, 128), jnp.float32)
    held = jax.ShapeDtypeStruct((n // 128, rows.shape[0], 128), jnp.float32)
    vmem = pl.BlockSpec(memory_space=pltpu.VMEM)
    return pl.pallas_call(
        functools.partial(gram_kernel, 1.0 / count),
        in_specs=[pl.BlockSpec(memory_space=pltpu.SMEM), pl.BlockSpec(memory_space=pl.ANY)],
        out_specs=[vmem] * 3,
        out_shape=[half, half, held],
        scratch_shapes=[
            pltpu.VMEM((n, 2 * n), jnp.float32),
            pltpu.VMEM((tall, 128), jnp.float32),
            pltpu.SemaphoreType.DMA((sum(TILES), n // 128)),
        ],
        cost_estimate=BRIEF,
        compiler_params=pltpu.CompilerParams(vmem_limit_bytes=40 * MIB),
        name="local_gram",
    )(place, rows)


def sum_gram(keep, give, prepared, send):
    size = lax.axis_size("wide") * lax.axis_size("slab")
    held = keep + exchange(give, AXES, 1)
    part = held.shape[0] // 4
    pieces = [held[k * part : (k + 1) * part] for k in range(4)]
    total = pieces[0]
    arrived = [exchange(pieces[k], AXES, 4 * k) for k in range(1, 4)]
    for piece in arrived:
        total = total + piece
    total = total + exchange(total, AXES, 2)
    total, prepared = lax.optimization_barrier((total, prepared))
    soon, more = send(prepared)
    mask = 16
    while mask < size:
        total = total + exchange(total, AXES, mask)
        mask *= 2
    mine = jnp.concatenate([total] + [exchange(total, AXES, 4 * k) for k in range(1, 4)])
    mine, soon = lax.optimization_barrier((mine, soon))
    return mine, exchange(mine, AXES, 1), soon, more


def row_of(x, p):
    return jnp.broadcast_to(x[p : p + 1, :], x.shape)


def column_of(x, k):
    return jnp.broadcast_to(x[:, k : k + 1], x.shape)


def total(terms):
    while len(terms) > 1:
        odd = terms[len(terms) & ~1 :]
        terms = [x + y for x, y in zip(terms[::2], terms[1::2], strict=False)] + odd
    return terms[0]


def invert_factor(work, result):
    n = work.shape[0]
    lane = lax.broadcasted_iota(jnp.int32, (8, n), 1)
    sub = lax.broadcasted_iota(jnp.int32, (8, n), 0)
    columns = [column_of(work[:8, :], k) for k in range(8)]
    for lo in range(0, n, 8):
        hi = lo + 8
        rows = work[lo:hi, :]
        if hi < n:
            rest = work[hi:, :]
            factors = [column_of(rest, lo + k) for k in range(8)]
            across = [column_of(rows, hi + k) for k in range(8)]
            later = [column_of(rest[:8], hi + k) for k in range(8)]
            under = [x[:8] for x in factors]
        rows = jnp.where((lane >= lo) & (lane < hi), (lane - lo == sub).astype(jnp.float32), rows)
        scaled = jnp.zeros((8, n), jnp.float32)
        for p in range(8):
            here = sub == p
            column = columns[p]
            pivot = row_of(column, p)
            inverse = 1.0 / pivot
            row = row_of(rows, p)
            scaled = jnp.where(here, row * lax.rsqrt(pivot), scaled)
            row = row * inverse
            rows = jnp.where(here, row, rows - column * row)
            for k in range(8 if hi < n else 0):
                if k == p:
                    continue
                entry = row_of(columns[k], p)
                if k == p + 1:
                    kept = jnp.where(here, 0.0, columns[k])
                    columns[k] = kept - jnp.where(here, -entry, column * entry) * inverse
                else:
                    columns[k] = jnp.where(here, entry * inverse, columns[k] - column * (entry * inverse))
                under[k] = under[k] - under[p] * (entry * inverse)
            if hi < n:
                columns[p] = jnp.where(here, inverse, -column * inverse)
                under[p] = -under[p] * inverse
            else:
                for k in range(p + 1, 8):
                    entry = row_of(columns[k], p) * inverse
                    columns[k] = jnp.where(here, entry, columns[k] - column * entry)
        result[lo:hi, :] = jnp.where(lane <= sub + lo, scaled, 0.0)
        if hi < n:
            columns = [
                later[k] + total([under[p] * row_of(across[k], p) for p in range(8)])
                for k in range(8)
            ]
            lane_rest = lax.broadcasted_iota(jnp.int32, rest.shape, 1)
            kept = jnp.where((lane_rest >= lo) & (lane_rest < hi), 0.0, rest)
            work[hi:, :] = kept - total(
                [factors[k] * jnp.broadcast_to(rows[k : k + 1, :], rest.shape) for k in range(8)]
            )


def sweep_kernel(
    sweeps, place_ref, mine_ref, other_ref, start_ref, block_ref, blocks, gram, gram_high, gram_low,
    ahead, work, factor,
):
    place = place_ref[0]
    part = mine_ref.shape[0] // 4
    for k in range(4):
        quarter = ((place >> 2) & 3) ^ k
        mine = pl.multiple_of(((place & 1) * 4 + quarter) * part, 8)
        theirs = pl.multiple_of(((1 - (place & 1)) * 4 + quarter) * part, 8)
        blocks[pl.ds(mine, part), :] = mine_ref[k * part : (k + 1) * part, :]
        blocks[pl.ds(theirs, part), :] = other_ref[k * part : (k + 1) * part, :]
    edge = 128
    for number, (i, j) in enumerate(upper_blocks(gram.shape[0] // edge)):
        block = blocks[number * edge : (number + 1) * edge, :]
        gram[i * edge : (i + 1) * edge, j * edge : (j + 1) * edge] = block
        if i != j:
            gram[j * edge : (j + 1) * edge, i * edge : (i + 1) * edge] = block.T

    gram_high[...], gram_low[...] = halves(gram[...])

    def by_gram(block):
        high, low = halves(block)
        both = dot(jnp.concatenate([high, low], axis=0), gram_high[...], NN)
        rank = block.shape[0]
        return both[:rank] + both[rank:] + dot(high, gram_low[...], NN)

    block_ref[...] = by_gram(start_ref[...].T)

    def sweep(_, carry):
        block = block_ref[...]
        work[...] = dot(block, block, NT, HIGHEST)
        ahead[...] = by_gram(block)
        invert_factor(work, factor)
        block_ref[...] = dot(factor[...], ahead[...], NN, HIGHEST)
        return carry

    lax.fori_loop(0, sweeps - 1, sweep, 0)


def iterate(place, mine, other, start):
    n, rank = start.shape
    vmem = pl.BlockSpec(memory_space=pltpu.VMEM)
    return pl.pallas_call(
        functools.partial(sweep_kernel, SWEEPS),
        in_specs=[pl.BlockSpec(memory_space=pltpu.SMEM), vmem, vmem, vmem],
        out_specs=vmem,
        out_shape=jax.ShapeDtypeStruct((rank, n), jnp.float32),
        scratch_shapes=[
            pltpu.VMEM((2 * mine.shape[0], 128), jnp.float32),
            pltpu.VMEM((n, n), jnp.float32),
            pltpu.VMEM((n, n), jnp.bfloat16),
            pltpu.VMEM((n, n), jnp.bfloat16),
            pltpu.VMEM((rank, n), jnp.float32),
            pltpu.VMEM((rank, rank), jnp.float32),
            pltpu.VMEM((rank, rank), jnp.float32),
        ],
        cost_estimate=BRIEF,
        compiler_params=pltpu.CompilerParams(vmem_limit_bytes=16 * MIB),
        name="iterate",
    )(place, mine, other, start)


def factor_kernel(block_ref, out_ref, work):
    block = block_ref[...]
    work[...] = dot(block, block, NT, HIGHEST)
    invert_factor(work, out_ref)


def last_factor(block):
    rank = block.shape[0]
    vmem = pl.BlockSpec(memory_space=pltpu.VMEM)
    return pl.pallas_call(
        factor_kernel,
        in_specs=[vmem],
        out_specs=vmem,
        out_shape=jax.ShapeDtypeStruct((rank, rank), jnp.float32),
        scratch_shapes=[pltpu.VMEM((rank, rank), jnp.float32)],
        cost_estimate=BRIEF,
        compiler_params=pltpu.CompilerParams(vmem_limit_bytes=16 * MIB),
        name="last_factor",
    )(block)


def weights(block_ref):
    return jnp.concatenate(halves(block_ref[...]), axis=0)


def split_product(high, low, both):
    rank = both.shape[0] // 2
    product = dot(high, both, NT)
    return product[:, :rank] + product[:, rank:] + dot(low, both[:rank], NT)


def halved_product(x, both):
    return split_product(*halves(x), both)


def pick(held, place_ref, rank, first, fibres, j):
    start = first * 8 + (place_ref[1] ^ rank) * (8 // SLABS) + j
    return side_by_side(held, pl.ds(start, fibres, stride=8))


def chunks_of(rank):
    return sum(count for to, _, count in EARLY if to == rank)


def prepare_kernel(place_ref, held, *refs):
    per = 8 // SLABS
    high_ref, low_ref = refs[-2:]
    chunk = held.shape[1] // 8 // CHUNKS
    for (rank, first, count), out in zip(EARLY, refs[:-2], strict=True):
        for j in range(per):
            rows = pick(held, place_ref, rank, first * chunk, count * chunk, j)
            for c in range(out.shape[0]):
                out[c, pl.ds(j, count * chunk, stride=per), :] = rows[:, c * 128 : (c + 1) * 128]
    begin = 0
    for rank in (1, *FAR):
        first = chunks_of(rank) * chunk
        fibres = CHUNKS * chunk - first
        for j in range(per):
            high, low = halves(pick(held, place_ref, rank, first, fibres, j))
            high_ref[begin : begin + fibres, :] = high
            low_ref[begin : begin + fibres, :] = low
            begin += fibres


def prepare(place, held):
    columns, rows, lanes = held.shape
    chunk = rows // SLABS // CHUNKS
    count = sum(CHUNKS - chunks_of(rank) for rank in (1, *FAR)) * chunk
    split = jax.ShapeDtypeStruct((count, columns * lanes), jnp.bfloat16)
    sent = [
        jax.ShapeDtypeStruct((columns, some * chunk, lanes), jnp.float32) for _, _, some in EARLY
    ]
    vmem = pl.BlockSpec(memory_space=pltpu.VMEM)
    return pl.pallas_call(
        prepare_kernel,
        in_specs=[pl.BlockSpec(memory_space=pltpu.SMEM), vmem],
        out_specs=[vmem] * (len(sent) + 2),
        out_shape=[*sent, split, split],
        cost_estimate=BRIEF,
        compiler_params=pltpu.CompilerParams(vmem_limit_bytes=16 * MIB),
        name="prepare",
    )(place, held)


def sent_kernel(high_ref, low_ref, block_ref, *outs):
    per = 8 // SLABS
    both = weights(block_ref)
    begin = 0
    for out in outs:
        fibres = out.shape[0] // per
        span = slice(begin, begin + fibres * per)
        product = split_product(high_ref[span, :], low_ref[span, :], both)
        for j in range(per):
            out[pl.ds(j, fibres, stride=per), :] = product[j * fibres : (j + 1) * fibres]
        begin += fibres * per


def project_sent(high, low, block):
    rank = block.shape[0]
    parts = [CHUNKS - chunks_of(to) for to in (1, *FAR)]
    sizes = [part * high.shape[0] // sum(parts) for part in parts]
    vmem = pl.BlockSpec(memory_space=pltpu.VMEM)
    return pl.pallas_call(
        sent_kernel,
        in_specs=[vmem] * 3,
        out_specs=[vmem] * 3,
        out_shape=[jax.ShapeDtypeStruct((size, rank), jnp.float32) for size in sizes],
        cost_estimate=BRIEF,
        compiler_params=pltpu.CompilerParams(vmem_limit_bytes=16 * MIB),
        name="project_sent",
    )(high, low, block)


def own_kernel(place_ref, held, block_ref, out):
    per = 8 // SLABS
    both = weights(block_ref)
    fibres = held.shape[1] // 8
    x = jnp.concatenate([pick(held, place_ref, 0, 0, fibres, j) for j in range(per)], axis=0)
    product = halved_product(x, both)
    for j in range(per):
        out[pl.ds(j, fibres, stride=per), :] = product[j * fibres : (j + 1) * fibres]


def project_own(place, held, block):
    vmem = pl.BlockSpec(memory_space=pltpu.VMEM)
    return pl.pallas_call(
        own_kernel,
        in_specs=[pl.BlockSpec(memory_space=pltpu.SMEM), vmem, vmem],
        out_specs=vmem,
        out_shape=jax.ShapeDtypeStruct((held.shape[1] // SLABS, block.shape[0]), jnp.float32),
        cost_estimate=BRIEF,
        compiler_params=pltpu.CompilerParams(vmem_limit_bytes=16 * MIB),
        name="project_own",
    )(place, held, block)


def arrived_kernel(block_ref, *refs):
    outs = refs[-len(FAR) :]
    both = weights(block_ref)
    begins = [0] * len(FAR)
    for (rank, _, _), x_ref in zip(EARLY, refs[: len(EARLY)], strict=True):
        k, size = FAR.index(rank), x_ref.shape[1]
        x = side_by_side(x_ref, slice(None))
        outs[k][begins[k] : begins[k] + size, :] = halved_product(x, both)
        begins[k] += size


def project_arrived(block, arrived):
    vmem = pl.BlockSpec(memory_space=pltpu.VMEM)
    chunk = arrived[0].shape[1] // EARLY[0][2]
    return pl.pallas_call(
        arrived_kernel,
        in_specs=[vmem] * (1 + len(arrived)),
        out_specs=[vmem] * len(FAR),
        out_shape=[
            jax.ShapeDtypeStruct((chunks_of(rank) * chunk, block.shape[0]), jnp.float32)
            for rank in FAR
        ],
        cost_estimate=BRIEF,
        compiler_params=pltpu.CompilerParams(vmem_limit_bytes=16 * MIB),
        name="project_arrived",
    )(block, *arrived)


def finish_kernel(ranks, firsts, place_ref, factor_ref, *refs):
    pieces = refs[: len(ranks)]
    out, *results, sems = refs[-2 - len(ranks) :]
    factor = factor_ref[...]
    per, size = out.shape[2], out.shape[3]
    sends = []
    for k, (rank, first, piece) in enumerate(zip(ranks, firsts, pieces, strict=True)):
        last = first + results[k].shape[0]
        begin = first
        while begin < last:
            length = min(per - begin % per, last - begin)
            span = pl.ds(begin - first, length)
            rows = piece[(begin - first) * size : (begin - first + length) * size, :]
            results[k][span] = dot(rows, factor, NT, HIGHEST).reshape(length, size, -1)
            send = pltpu.make_async_copy(
                results[k].at[span],
                out.at[begin // per, place_ref[1] ^ rank, pl.ds(begin % per, length)],
                sems.at[k, begin // per],
            )
            send.start()
            sends.append(send)
            begin += length
    for send in sends:
        send.wait()


def finish(place, factor, pieces, ranks, firsts, into, name):
    shape = into if isinstance(into, tuple) else into.shape
    size, rank = shape[3:]
    vmem = pl.BlockSpec(memory_space=pltpu.VMEM)
    in_specs = [pl.BlockSpec(memory_space=pltpu.SMEM)] + [vmem] * (1 + len(pieces))
    operands = [place, factor, *pieces]
    aliases = {}
    if not isinstance(into, tuple):
        aliases = {len(operands): 0}
        in_specs.append(pl.BlockSpec(memory_space=pl.ANY))
        operands.append(into)
    return pl.pallas_call(
        functools.partial(finish_kernel, ranks, firsts),
        in_specs=in_specs,
        out_specs=pl.BlockSpec(memory_space=pl.ANY),
        out_shape=jax.ShapeDtypeStruct(shape, jnp.float32),
        scratch_shapes=[
            pltpu.VMEM((piece.shape[0] // size, size, rank), jnp.float32) for piece in pieces
        ]
        + [pltpu.SemaphoreType.DMA((len(pieces), shape[0]))],
        input_output_aliases=aliases,
        cost_estimate=BRIEF,
        compiler_params=pltpu.CompilerParams(vmem_limit_bytes=16 * MIB),
        name=name,
    )(*operands)


def per_device(fields, start_basis):
    nv, n2, n3, n1 = fields.shape
    slabs = lax.axis_size("slab")
    slab = lax.axis_index("slab")
    place = jnp.stack([lax.axis_index("wide") * slabs + slab, slab]).astype(jnp.int32)
    rows = fields.reshape(-1, n1)
    count = float(rows.shape[0] * lax.axis_size("wide") * slabs)
    def to_far(some, ranks):
        return [exchange(x, "slab", rank) for x, rank in zip(some, ranks, strict=True)]

    def send(prepared):
        *sent, high, low = prepared
        ranks = [rank for rank, _, _ in EARLY]
        return [*to_far(sent[:1], ranks[:1]), high, low], to_far(sent[1:], ranks[1:])

    keep, give, held = local_gram(place, rows, count)
    prepared = prepare(place, held)
    mine, other, (soon, high, low), later = sum_gram(keep, give, prepared, send)
    block = iterate(place, mine, other, start_basis)

    block, *arrived = lax.optimization_barrier((block, soon, *later))
    near, *far = project_sent(high, low, block)
    block, near, *far = lax.optimization_barrier((block, near, *far))
    far = to_far(far, FAR)
    near = exchange(near, "slab", 1)
    own = project_own(place, held, block)
    arrived = project_arrived(block, arrived)
    factor = last_factor(block)

    per = CHUNKS // nv
    out = (nv, slabs, per, n2 * n3 // slabs // per, block.shape[0])
    late = [chunks_of(rank) for rank in FAR]
    out = finish(place, factor, arrived, FAR, (0, 0), out, "finish_arrived")
    out = finish(place, factor, far[:1], FAR[:1], late[:1], out, "finish_first_far")
    out = finish(place, factor, [own, near], (0, 1), (0, 0), out, "finish_near")
    out = finish(place, factor, far[1:], FAR[1:], late[1:], out, "finish_last_far")
    return out.reshape(nv, n2 * slabs, n3 // slabs, out.shape[-1])


def solution(mesh):
    in_specs = (P(None, "slab", "wide", None), P())
    out_specs = P(None, None, ("wide", "slab"), None)
    return jax.shard_map(
        per_device, mesh=mesh, in_specs=in_specs, out_specs=out_specs, check_vma=False
    )
```

```python
import functools

import jax
import jax.numpy as jnp
from jax import lax
from jax.experimental import pallas as pl
from jax.experimental.pallas import tpu as pltpu
from jax.sharding import PartitionSpec as P

SWEEPS = 4
SLABS = 4
CHUNKS = 16
EARLY = ((2, 0, 4), (3, 0, 4))
FAR = (2, 3)
TILES = (1, 1, 2, 2, 2)
AXES = ("wide", "slab")
MIB = 1 << 20
HIGHEST = lax.Precision.HIGHEST
NN = (((1,), (0,)), ((), ()))
NT = (((1,), (1,)), ((), ()))
TN = (((0,), (0,)), ((), ()))
BRIEF = pl.CostEstimate(flops=1, bytes_accessed=1, transcendentals=0)


def dot(a, b, dims, precision=None):
    return lax.dot_general(a, b, dims, precision=precision, preferred_element_type=jnp.float32)


def halves(x):
    high = x.astype(jnp.bfloat16)
    return high, (x - high.astype(jnp.float32)).astype(jnp.bfloat16)


def split_dot(a, b):
    a_high, a_low = halves(a)
    b_high, b_low = halves(b)
    both = dot(jnp.concatenate([a_high, a_low], axis=0), b_high, NN)
    rows = a.shape[0]
    return both[:rows] + both[rows:] + dot(a_high, b_low, NN)


def exchange(value, axes, mask):
    size = 1
    for axis in axes if isinstance(axes, tuple) else (axes,):
        size *= lax.axis_size(axis)
    return lax.ppermute(value, axes, [(i, i ^ mask) for i in range(size)])


EDGE = 128


def upper_blocks(n):
    return [(i, j) for i in range(n // EDGE) for j in range(i + 1, n // EDGE)]


def packed_rows(n):
    return pl.cdiv((len(upper_blocks(n)) + n // EDGE // 2) * EDGE + 8, 64) * 64


def span(number):
    return slice(number * EDGE, (number + 1) * EDGE)


def block_indices():
    return [lax.broadcasted_iota(jnp.int32, (EDGE, EDGE), axis) for axis in (0, 1)]


def copies(x_ref, held, sems):
    tile = held.shape[1] // sems.shape[0]
    return [
        [
            pltpu.make_async_copy(
                x_ref.at[pl.ds(i * tile, tile), pl.ds(c * 128, 128)],
                held.at[c, pl.ds(i * tile, tile)],
                sems.at[i, c],
            )
            for c in range(held.shape[0])
        ]
        for i in range(sems.shape[0])
    ]


def side_by_side(ref, rows):
    return jnp.concatenate([ref[c, rows, :] for c in range(ref.shape[0])], axis=1)


def gram_kernel(scale, place_ref, x_ref, *refs):
    keep_ref, give_ref, held, acc, whole, sems = refs
    n = held.shape[0] * held.shape[2]
    half = n // 2
    arrivals = copies(x_ref, held, sems)
    for arrival in arrivals:
        for copy in arrival:
            copy.start()
    tile = held.shape[1] // len(arrivals)
    first = 0
    for count in TILES:
        for arrival in arrivals[first : first + count]:
            for copy in arrival:
                copy.wait()
        high, low = halves(side_by_side(held, pl.ds(first * tile, count * tile)))
        left = dot(high[:, :half], jnp.concatenate([high, low], axis=1), TN)
        right = dot(high[:, half:], jnp.concatenate([high[:, half:], low], axis=1), TN)
        if first == 0:
            acc[:half, :] = left
            acc[half:, half:] = right
        else:
            acc[:half, :] += left
            acc[half:, half:] += right
        first += count

    def block(i, j):
        cross = acc[span(i), n + j * EDGE : n + (j + 1) * EDGE]
        other = acc[span(j), n + i * EDGE : n + (i + 1) * EDGE]
        return (acc[span(i), span(j)] + cross + other.T) * scale

    above = upper_blocks(n)
    for number, (i, j) in enumerate(above):
        whole[span(number), :] = block(i, j)
    row, column = block_indices()
    tail = len(above) + n // EDGE // 2
    whole[tail * EDGE :, :] = jnp.zeros((whole.shape[0] - tail * EDGE, EDGE), jnp.float32)
    for pair in range(n // EDGE // 2):
        first, second = block(2 * pair, 2 * pair), block(2 * pair + 1, 2 * pair + 1)
        whole[span(len(above) + pair), :] = jnp.where(row <= column, first, second)
        diagonal = jnp.sum(jnp.where(row == column, second, 0.0), axis=0, keepdims=True)
        whole[tail * EDGE + pair : tail * EDGE + pair + 1, :] = diagonal
    place = place_ref[0]
    part = keep_ref.shape[0] // 4
    for k in range(4):
        quarter = ((place >> 2) & 3) ^ k
        mine = pl.multiple_of(((place & 1) * 4 + quarter) * part, 8)
        theirs = pl.multiple_of(((1 - (place & 1)) * 4 + quarter) * part, 8)
        keep_ref[k * part : (k + 1) * part, :] = whole[pl.ds(mine, part), :]
        give_ref[k * part : (k + 1) * part, :] = whole[pl.ds(theirs, part), :]


def local_gram(place, rows, count):
    n = rows.shape[1]
    tall = packed_rows(n)
    half = jax.ShapeDtypeStruct((tall // 2, 128), jnp.float32)
    held = jax.ShapeDtypeStruct((n // 128, rows.shape[0], 128), jnp.float32)
    vmem = pl.BlockSpec(memory_space=pltpu.VMEM)
    return pl.pallas_call(
        functools.partial(gram_kernel, 1.0 / count),
        in_specs=[pl.BlockSpec(memory_space=pltpu.SMEM), pl.BlockSpec(memory_space=pl.ANY)],
        out_specs=[vmem] * 3,
        out_shape=[half, half, held],
        scratch_shapes=[
            pltpu.VMEM((n, 2 * n), jnp.float32),
            pltpu.VMEM((tall, 128), jnp.float32),
            pltpu.SemaphoreType.DMA((sum(TILES), n // 128)),
        ],
        cost_estimate=BRIEF,
        compiler_params=pltpu.CompilerParams(vmem_limit_bytes=40 * MIB),
        name="local_gram",
    )(place, rows)


def sum_gram(keep, give, prepared, send):
    size = lax.axis_size("wide") * lax.axis_size("slab")
    held = keep + exchange(give, AXES, 1)
    part = held.shape[0] // 4
    pieces = [held[k * part : (k + 1) * part] for k in range(4)]
    total = pieces[0]
    arrived = [exchange(pieces[k], AXES, 4 * k) for k in range(1, 4)]
    for piece in arrived:
        total = total + piece
    total = total + exchange(total, AXES, 2)
    total, prepared = lax.optimization_barrier((total, prepared))
    soon, more = send(prepared)
    mask = 16
    while mask < size:
        total = total + exchange(total, AXES, mask)
        mask *= 2
    mine = jnp.concatenate([total] + [exchange(total, AXES, 4 * k) for k in range(1, 4)])
    mine, soon = lax.optimization_barrier((mine, soon))
    return mine, exchange(mine, AXES, 1), soon, more


def row_of(x, p):
    return jnp.broadcast_to(x[p : p + 1, :], x.shape)


def column_of(x, k):
    return jnp.broadcast_to(x[:, k : k + 1], x.shape)


def total(terms):
    while len(terms) > 1:
        odd = terms[len(terms) & ~1 :]
        terms = [x + y for x, y in zip(terms[::2], terms[1::2], strict=False)] + odd
    return terms[0]


def invert_factor(work, result):
    n = work.shape[0]
    lane = lax.broadcasted_iota(jnp.int32, (8, n), 1)
    sub = lax.broadcasted_iota(jnp.int32, (8, n), 0)
    columns = [column_of(work[:8, :], k) for k in range(8)]
    for lo in range(0, n, 8):
        hi = lo + 8
        rows = work[lo:hi, :]
        if hi < n:
            rest = work[hi:, :]
            factors = [column_of(rest, lo + k) for k in range(8)]
            across = [column_of(rows, hi + k) for k in range(8)]
            later = [column_of(rest[:8], hi + k) for k in range(8)]
            under = [x[:8] for x in factors]
        rows = jnp.where((lane >= lo) & (lane < hi), (lane - lo == sub).astype(jnp.float32), rows)
        scaled = jnp.zeros((8, n), jnp.float32)
        for p in range(8):
            here = sub == p
            column = columns[p]
            pivot = row_of(column, p)
            inverse = 1.0 / pivot
            row = row_of(rows, p)
            scaled = jnp.where(here, row * lax.rsqrt(pivot), scaled)
            row = row * inverse
            rows = jnp.where(here, row, rows - column * row)
            for k in range(8 if hi < n else 0):
                if k == p:
                    continue
                entry = row_of(columns[k], p)
                if k == p + 1:
                    kept = jnp.where(here, 0.0, columns[k])
                    columns[k] = kept - jnp.where(here, -entry, column * entry) * inverse
                else:
                    columns[k] = jnp.where(here, entry * inverse, columns[k] - column * (entry * inverse))
                under[k] = under[k] - under[p] * (entry * inverse)
            if hi < n:
                columns[p] = jnp.where(here, inverse, -column * inverse)
                under[p] = -under[p] * inverse
            else:
                for k in range(p + 1, 8):
                    entry = row_of(columns[k], p) * inverse
                    columns[k] = jnp.where(here, entry, columns[k] - column * entry)
        result[lo:hi, :] = jnp.where(lane <= sub + lo, scaled, 0.0)
        if hi < n:
            columns = [
                later[k] + total([under[p] * row_of(across[k], p) for p in range(8)])
                for k in range(8)
            ]
            lane_rest = lax.broadcasted_iota(jnp.int32, rest.shape, 1)
            kept = jnp.where((lane_rest >= lo) & (lane_rest < hi), 0.0, rest)
            work[hi:, :] = kept - total(
                [factors[k] * jnp.broadcast_to(rows[k : k + 1, :], rest.shape) for k in range(8)]
            )


def sweep_kernel(
    sweeps, place_ref, mine_ref, other_ref, start_ref, block_ref, blocks, gram, gram_high, gram_low,
    ahead, work, factor,
):
    place = place_ref[0]
    part = mine_ref.shape[0] // 4
    for k in range(4):
        quarter = ((place >> 2) & 3) ^ k
        mine = pl.multiple_of(((place & 1) * 4 + quarter) * part, 8)
        theirs = pl.multiple_of(((1 - (place & 1)) * 4 + quarter) * part, 8)
        blocks[pl.ds(mine, part), :] = mine_ref[k * part : (k + 1) * part, :]
        blocks[pl.ds(theirs, part), :] = other_ref[k * part : (k + 1) * part, :]
    n = gram.shape[0]
    above = upper_blocks(n)
    for number, (i, j) in enumerate(above):
        block = blocks[span(number), :]
        gram[span(i), span(j)] = block
        gram[span(j), span(i)] = block.T
    row, column = block_indices()
    tail = len(above) + n // EDGE // 2
    for pair in range(n // EDGE // 2):
        block = blocks[span(len(above) + pair), :]
        turned = block.T
        first, second = span(2 * pair), span(2 * pair + 1)
        diagonal = blocks[tail * EDGE + pair : tail * EDGE + pair + 1, :]
        gram[first, first] = jnp.where(row <= column, block, turned)
        gram[second, second] = jnp.where(
            row == column, diagonal, jnp.where(row > column, block, turned)
        )
    gram_high[...], gram_low[...] = halves(gram[...])

    def by_gram(block):
        high, low = halves(block)
        both = dot(jnp.concatenate([high, low], axis=0), gram_high[...], NN)
        rank = block.shape[0]
        return both[:rank] + both[rank:] + dot(high, gram_low[...], NN)

    block_ref[...] = by_gram(start_ref[...].T)

    def sweep(_, carry):
        block = block_ref[...]
        work[...] = dot(block, block, NT, HIGHEST)
        ahead[...] = by_gram(block)
        invert_factor(work, factor)
        block_ref[...] = split_dot(factor[...], ahead[...])
        return carry

    lax.fori_loop(0, sweeps - 1, sweep, 0)


def iterate(place, mine, other, start):
    n, rank = start.shape
    vmem = pl.BlockSpec(memory_space=pltpu.VMEM)
    return pl.pallas_call(
        functools.partial(sweep_kernel, SWEEPS),
        in_specs=[pl.BlockSpec(memory_space=pltpu.SMEM), vmem, vmem, vmem],
        out_specs=vmem,
        out_shape=jax.ShapeDtypeStruct((rank, n), jnp.float32),
        scratch_shapes=[
            pltpu.VMEM((2 * mine.shape[0], 128), jnp.float32),
            pltpu.VMEM((n, n), jnp.float32),
            pltpu.VMEM((n, n), jnp.bfloat16),
            pltpu.VMEM((n, n), jnp.bfloat16),
            pltpu.VMEM((rank, n), jnp.float32),
            pltpu.VMEM((rank, rank), jnp.float32),
            pltpu.VMEM((rank, rank), jnp.float32),
        ],
        cost_estimate=BRIEF,
        compiler_params=pltpu.CompilerParams(vmem_limit_bytes=16 * MIB),
        name="iterate",
    )(place, mine, other, start)


def factor_kernel(block_ref, out_ref, work):
    block = block_ref[...]
    work[...] = dot(block, block, NT, HIGHEST)
    invert_factor(work, out_ref)


def last_factor(block):
    rank = block.shape[0]
    vmem = pl.BlockSpec(memory_space=pltpu.VMEM)
    return pl.pallas_call(
        factor_kernel,
        in_specs=[vmem],
        out_specs=vmem,
        out_shape=jax.ShapeDtypeStruct((rank, rank), jnp.float32),
        scratch_shapes=[pltpu.VMEM((rank, rank), jnp.float32)],
        cost_estimate=BRIEF,
        compiler_params=pltpu.CompilerParams(vmem_limit_bytes=16 * MIB),
        name="last_factor",
    )(block)


def weights(block_ref):
    return jnp.concatenate(halves(block_ref[...]), axis=0)


def split_product(high, low, both):
    rank = both.shape[0] // 2
    product = dot(high, both, NT)
    return product[:, :rank] + product[:, rank:] + dot(low, both[:rank], NT)


def halved_product(x, both):
    return split_product(*halves(x), both)


def pick(held, place_ref, rank, first, fibres, j):
    start = first * 8 + (place_ref[1] ^ rank) * (8 // SLABS) + j
    return side_by_side(held, pl.ds(start, fibres, stride=8))


def chunks_of(rank):
    return sum(count for to, _, count in EARLY if to == rank)


def prepare_kernel(place_ref, held, *refs):
    per = 8 // SLABS
    high_ref, low_ref = refs[-2:]
    chunk = held.shape[1] // 8 // CHUNKS
    for (rank, first, count), out in zip(EARLY, refs[:-2], strict=True):
        for j in range(per):
            rows = pick(held, place_ref, rank, first * chunk, count * chunk, j)
            for c in range(out.shape[0]):
                out[c, pl.ds(j, count * chunk, stride=per), :] = rows[:, c * 128 : (c + 1) * 128]
    begin = 0
    for rank in (1, *FAR):
        first = chunks_of(rank) * chunk
        fibres = CHUNKS * chunk - first
        for j in range(per):
            high, low = halves(pick(held, place_ref, rank, first, fibres, j))
            high_ref[begin : begin + fibres, :] = high
            low_ref[begin : begin + fibres, :] = low
            begin += fibres


def prepare(place, held):
    columns, rows, lanes = held.shape
    chunk = rows // SLABS // CHUNKS
    count = sum(CHUNKS - chunks_of(rank) for rank in (1, *FAR)) * chunk
    split = jax.ShapeDtypeStruct((count, columns * lanes), jnp.bfloat16)
    sent = [
        jax.ShapeDtypeStruct((columns, some * chunk, lanes), jnp.float32) for _, _, some in EARLY
    ]
    vmem = pl.BlockSpec(memory_space=pltpu.VMEM)
    return pl.pallas_call(
        prepare_kernel,
        in_specs=[pl.BlockSpec(memory_space=pltpu.SMEM), vmem],
        out_specs=[vmem] * (len(sent) + 2),
        out_shape=[*sent, split, split],
        cost_estimate=BRIEF,
        compiler_params=pltpu.CompilerParams(vmem_limit_bytes=16 * MIB),
        name="prepare",
    )(place, held)


def sent_kernel(high_ref, low_ref, block_ref, *outs):
    per = 8 // SLABS
    both = weights(block_ref)
    begin = 0
    for out in outs:
        fibres = out.shape[0] // per
        part = slice(begin, begin + fibres * per)
        product = split_product(high_ref[part, :], low_ref[part, :], both)
        for j in range(per):
            out[pl.ds(j, fibres, stride=per), :] = product[j * fibres : (j + 1) * fibres]
        begin += fibres * per


def project_sent(high, low, block):
    rank = block.shape[0]
    parts = [CHUNKS - chunks_of(to) for to in (1, *FAR)]
    sizes = [part * high.shape[0] // sum(parts) for part in parts]
    vmem = pl.BlockSpec(memory_space=pltpu.VMEM)
    return pl.pallas_call(
        sent_kernel,
        in_specs=[vmem] * 3,
        out_specs=[vmem] * 3,
        out_shape=[jax.ShapeDtypeStruct((size, rank), jnp.float32) for size in sizes],
        cost_estimate=BRIEF,
        compiler_params=pltpu.CompilerParams(vmem_limit_bytes=16 * MIB),
        name="project_sent",
    )(high, low, block)


def own_kernel(place_ref, held, block_ref, out):
    per = 8 // SLABS
    both = weights(block_ref)
    fibres = held.shape[1] // 8
    x = jnp.concatenate([pick(held, place_ref, 0, 0, fibres, j) for j in range(per)], axis=0)
    product = halved_product(x, both)
    for j in range(per):
        out[pl.ds(j, fibres, stride=per), :] = product[j * fibres : (j + 1) * fibres]


def project_own(place, held, block):
    vmem = pl.BlockSpec(memory_space=pltpu.VMEM)
    return pl.pallas_call(
        own_kernel,
        in_specs=[pl.BlockSpec(memory_space=pltpu.SMEM), vmem, vmem],
        out_specs=vmem,
        out_shape=jax.ShapeDtypeStruct((held.shape[1] // SLABS, block.shape[0]), jnp.float32),
        cost_estimate=BRIEF,
        compiler_params=pltpu.CompilerParams(vmem_limit_bytes=16 * MIB),
        name="project_own",
    )(place, held, block)


def arrived_kernel(block_ref, *refs):
    outs = refs[-len(FAR) :]
    both = weights(block_ref)
    begins = [0] * len(FAR)
    for (rank, _, _), x_ref in zip(EARLY, refs[: len(EARLY)], strict=True):
        k, size = FAR.index(rank), x_ref.shape[1]
        x = side_by_side(x_ref, slice(None))
        outs[k][begins[k] : begins[k] + size, :] = halved_product(x, both)
        begins[k] += size


def project_arrived(block, arrived):
    vmem = pl.BlockSpec(memory_space=pltpu.VMEM)
    chunk = arrived[0].shape[1] // EARLY[0][2]
    return pl.pallas_call(
        arrived_kernel,
        in_specs=[vmem] * (1 + len(arrived)),
        out_specs=[vmem] * len(FAR),
        out_shape=[
            jax.ShapeDtypeStruct((chunks_of(rank) * chunk, block.shape[0]), jnp.float32)
            for rank in FAR
        ],
        cost_estimate=BRIEF,
        compiler_params=pltpu.CompilerParams(vmem_limit_bytes=16 * MIB),
        name="project_arrived",
    )(block, *arrived)


def finish_kernel(ranks, firsts, place_ref, factor_ref, *refs):
    pieces = refs[: len(ranks)]
    out, *results, sems = refs[-2 - len(ranks) :]
    factor = factor_ref[...]
    per, size = out.shape[2], out.shape[3]
    sends = []
    for k, (rank, first, piece) in enumerate(zip(ranks, firsts, pieces, strict=True)):
        last = first + results[k].shape[0]
        begin = first
        while begin < last:
            length = min(per - begin % per, last - begin)
            done = pl.ds(begin - first, length)
            rows = piece[(begin - first) * size : (begin - first + length) * size, :]
            results[k][done] = dot(rows, factor, NT, HIGHEST).reshape(length, size, -1)
            send = pltpu.make_async_copy(
                results[k].at[done],
                out.at[begin // per, place_ref[1] ^ rank, pl.ds(begin % per, length)],
                sems.at[k, begin // per],
            )
            send.start()
            sends.append(send)
            begin += length
    for send in sends:
        send.wait()


def finish(place, factor, pieces, ranks, firsts, into, name):
    shape = into if isinstance(into, tuple) else into.shape
    size, rank = shape[3:]
    vmem = pl.BlockSpec(memory_space=pltpu.VMEM)
    in_specs = [pl.BlockSpec(memory_space=pltpu.SMEM)] + [vmem] * (1 + len(pieces))
    operands = [place, factor, *pieces]
    aliases = {}
    if not isinstance(into, tuple):
        aliases = {len(operands): 0}
        in_specs.append(pl.BlockSpec(memory_space=pl.ANY))
        operands.append(into)
    return pl.pallas_call(
        functools.partial(finish_kernel, ranks, firsts),
        in_specs=in_specs,
        out_specs=pl.BlockSpec(memory_space=pl.ANY),
        out_shape=jax.ShapeDtypeStruct(shape, jnp.float32),
        scratch_shapes=[
            pltpu.VMEM((piece.shape[0] // size, size, rank), jnp.float32) for piece in pieces
        ]
        + [pltpu.SemaphoreType.DMA((len(pieces), shape[0]))],
        input_output_aliases=aliases,
        cost_estimate=BRIEF,
        compiler_params=pltpu.CompilerParams(vmem_limit_bytes=16 * MIB),
        name=name,
    )(*operands)


def per_device(fields, start_basis):
    nv, n2, n3, n1 = fields.shape
    slabs = lax.axis_size("slab")
    slab = lax.axis_index("slab")
    place = jnp.stack([lax.axis_index("wide") * slabs + slab, slab]).astype(jnp.int32)
    rows = fields.reshape(-1, n1)
    count = float(rows.shape[0] * lax.axis_size("wide") * slabs)
    def to_far(some, ranks):
        return [exchange(x, "slab", rank) for x, rank in zip(some, ranks, strict=True)]

    def send(prepared):
        *sent, high, low = prepared
        ranks = [rank for rank, _, _ in EARLY]
        return [high, low], to_far(sent, ranks)

    keep, give, held = local_gram(place, rows, count)
    prepared = prepare(place, held)
    mine, other, (high, low), arrived = sum_gram(keep, give, prepared, send)
    block = iterate(place, mine, other, start_basis)

    block, *arrived = lax.optimization_barrier((block, *arrived))
    near, *far = project_sent(high, low, block)
    block, near, *far = lax.optimization_barrier((block, near, *far))
    far = to_far(far, FAR)
    near = exchange(near, "slab", 1)
    own = project_own(place, held, block)
    arrived = project_arrived(block, arrived)
    factor = last_factor(block)

    per = CHUNKS // nv
    out = (nv, slabs, per, n2 * n3 // slabs // per, block.shape[0])
    late = [chunks_of(rank) for rank in FAR]
    out = finish(place, factor, arrived, FAR, (0, 0), out, "finish_arrived")
    out = finish(place, factor, far[:1], FAR[:1], late[:1], out, "finish_first_far")
    out = finish(place, factor, [own, near], (0, 1), (0, 0), out, "finish_near")
    out = finish(place, factor, far[1:], FAR[1:], late[1:], out, "finish_last_far")
    return out.reshape(nv, n2 * slabs, n3 // slabs, out.shape[-1])


def solution(mesh):
    in_specs = (P(None, "slab", "wide", None), P())
    out_specs = P(None, None, ("wide", "slab"), None)
    return jax.shard_map(
        per_device, mesh=mesh, in_specs=in_specs, out_specs=out_specs, check_vma=False
    )
```

```python
import functools

import jax
import jax.numpy as jnp
from jax import lax
from jax.experimental import pallas as pl
from jax.experimental.pallas import tpu as pltpu
from jax.sharding import PartitionSpec as P

SWEEPS = 4
SLABS = 4
CHUNKS = 16
EARLY = ((2, 0, 4), (3, 0, 4))
FAR = (2, 3)
TILES = (1, 1, 2, 2, 2)
AXES = ("wide", "slab")
MIB = 1 << 20
HIGHEST = lax.Precision.HIGHEST
NN = (((1,), (0,)), ((), ()))
NT = (((1,), (1,)), ((), ()))
TN = (((0,), (0,)), ((), ()))
BRIEF = pl.CostEstimate(flops=1, bytes_accessed=1, transcendentals=0)


def dot(a, b, dims, precision=None):
    return lax.dot_general(a, b, dims, precision=precision, preferred_element_type=jnp.float32)


def halves(x):
    high = x.astype(jnp.bfloat16)
    return high, (x - high.astype(jnp.float32)).astype(jnp.bfloat16)


def split_dot(a, b):
    a_high, a_low = halves(a)
    b_high, b_low = halves(b)
    both = dot(jnp.concatenate([a_high, a_low], axis=0), b_high, NN)
    rows = a.shape[0]
    return both[:rows] + both[rows:] + dot(a_high, b_low, NN)


def exchange(value, axes, mask):
    size = 1
    for axis in axes if isinstance(axes, tuple) else (axes,):
        size *= lax.axis_size(axis)
    return lax.ppermute(value, axes, [(i, i ^ mask) for i in range(size)])


EDGE = 128


def upper_blocks(n):
    return [(i, j) for i in range(n // EDGE) for j in range(i + 1, n // EDGE)]


def packed_rows(n):
    return pl.cdiv((len(upper_blocks(n)) + n // EDGE // 2) * EDGE + 8, 64) * 64


def span(number):
    return slice(number * EDGE, (number + 1) * EDGE)


def block_indices():
    return [lax.broadcasted_iota(jnp.int32, (EDGE, EDGE), axis) for axis in (0, 1)]


def copies(x_ref, held, sems):
    tile = held.shape[1] // sems.shape[0]
    return [
        [
            pltpu.make_async_copy(
                x_ref.at[pl.ds(i * tile, tile), pl.ds(c * 128, 128)],
                held.at[c, pl.ds(i * tile, tile)],
                sems.at[i, c],
            )
            for c in range(held.shape[0])
        ]
        for i in range(sems.shape[0])
    ]


def side_by_side(ref, rows):
    return jnp.concatenate([ref[c, rows, :] for c in range(ref.shape[0])], axis=1)


def gram_kernel(scale, place_ref, x_ref, *refs):
    keep_ref, give_ref, held, acc, whole, sems = refs
    n = held.shape[0] * held.shape[2]
    half = n // 2
    arrivals = copies(x_ref, held, sems)
    for arrival in arrivals:
        for copy in arrival:
            copy.start()
    tile = held.shape[1] // len(arrivals)
    first = 0
    for count in TILES:
        for arrival in arrivals[first : first + count]:
            for copy in arrival:
                copy.wait()
        high, low = halves(side_by_side(held, pl.ds(first * tile, count * tile)))
        left = dot(high[:, :half], jnp.concatenate([high, low], axis=1), TN)
        right = dot(high[:, half:], jnp.concatenate([high[:, half:], low], axis=1), TN)
        if first == 0:
            acc[:half, :] = left
            acc[half:, half:] = right
        else:
            acc[:half, :] += left
            acc[half:, half:] += right
        first += count

    def block(i, j):
        cross = acc[span(i), n + j * EDGE : n + (j + 1) * EDGE]
        other = acc[span(j), n + i * EDGE : n + (i + 1) * EDGE]
        return (acc[span(i), span(j)] + cross + other.T) * scale

    above = upper_blocks(n)
    for number, (i, j) in enumerate(above):
        whole[span(number), :] = block(i, j)
    row, column = block_indices()
    tail = len(above) + n // EDGE // 2
    whole[tail * EDGE :, :] = jnp.zeros((whole.shape[0] - tail * EDGE, EDGE), jnp.float32)
    for pair in range(n // EDGE // 2):
        first, second = block(2 * pair, 2 * pair), block(2 * pair + 1, 2 * pair + 1)
        whole[span(len(above) + pair), :] = jnp.where(row <= column, first, second)
        diagonal = jnp.sum(jnp.where(row == column, second, 0.0), axis=0, keepdims=True)
        whole[tail * EDGE + pair : tail * EDGE + pair + 1, :] = diagonal
    place = place_ref[0]
    part = keep_ref.shape[0] // 4
    for k in range(4):
        quarter = ((place >> 2) & 3) ^ k
        mine = pl.multiple_of(((place & 1) * 4 + quarter) * part, 8)
        theirs = pl.multiple_of(((1 - (place & 1)) * 4 + quarter) * part, 8)
        keep_ref[k * part : (k + 1) * part, :] = whole[pl.ds(mine, part), :]
        give_ref[k * part : (k + 1) * part, :] = whole[pl.ds(theirs, part), :]


def local_gram(place, rows, count):
    n = rows.shape[1]
    tall = packed_rows(n)
    half = jax.ShapeDtypeStruct((tall // 2, 128), jnp.float32)
    held = jax.ShapeDtypeStruct((n // 128, rows.shape[0], 128), jnp.float32)
    vmem = pl.BlockSpec(memory_space=pltpu.VMEM)
    return pl.pallas_call(
        functools.partial(gram_kernel, 1.0 / count),
        in_specs=[pl.BlockSpec(memory_space=pltpu.SMEM), pl.BlockSpec(memory_space=pl.ANY)],
        out_specs=[vmem] * 3,
        out_shape=[half, half, held],
        scratch_shapes=[
            pltpu.VMEM((n, 2 * n), jnp.float32),
            pltpu.VMEM((tall, 128), jnp.float32),
            pltpu.SemaphoreType.DMA((sum(TILES), n // 128)),
        ],
        cost_estimate=BRIEF,
        compiler_params=pltpu.CompilerParams(vmem_limit_bytes=40 * MIB),
        name="local_gram",
    )(place, rows)


def sum_gram(keep, give, prepared, send):
    size = lax.axis_size("wide") * lax.axis_size("slab")
    held = keep + exchange(give, AXES, 1)
    part = held.shape[0] // 4
    pieces = [held[k * part : (k + 1) * part] for k in range(4)]
    total = pieces[0]
    arrived = [exchange(pieces[k], AXES, 4 * k) for k in range(1, 4)]
    for piece in arrived:
        total = total + piece
    total = total + exchange(total, AXES, 2)
    total, prepared = lax.optimization_barrier((total, prepared))
    soon, more = send(prepared)
    mask = 16
    while mask < size:
        total = total + exchange(total, AXES, mask)
        mask *= 2
    mine = jnp.concatenate([total] + [exchange(total, AXES, 4 * k) for k in range(1, 4)])
    mine, soon = lax.optimization_barrier((mine, soon))
    return mine, exchange(mine, AXES, 1), soon, more


def row_of(x, p):
    return jnp.broadcast_to(x[p : p + 1, :], x.shape)


def column_of(x, k):
    return jnp.broadcast_to(x[:, k : k + 1], x.shape)


def total(terms):
    while len(terms) > 1:
        odd = terms[len(terms) & ~1 :]
        terms = [x + y for x, y in zip(terms[::2], terms[1::2], strict=False)] + odd
    return terms[0]


def invert_factor(work, result):
    n = work.shape[0]
    lane = lax.broadcasted_iota(jnp.int32, (8, n), 1)
    sub = lax.broadcasted_iota(jnp.int32, (8, n), 0)
    columns = [column_of(work[:8, :], k) for k in range(8)]
    for lo in range(0, n, 8):
        hi = lo + 8
        rows = work[lo:hi, :]
        if hi < n:
            rest = work[hi:, :]
            factors = [column_of(rest, lo + k) for k in range(8)]
            across = [column_of(rows, hi + k) for k in range(8)]
            later = [column_of(rest[:8], hi + k) for k in range(8)]
            under = [x[:8] for x in factors]
        rows = jnp.where((lane >= lo) & (lane < hi), (lane - lo == sub).astype(jnp.float32), rows)
        scaled = jnp.zeros((8, n), jnp.float32)
        for p in range(8):
            here = sub == p
            column = columns[p]
            pivot = row_of(column, p)
            inverse = 1.0 / pivot
            row = row_of(rows, p)
            scaled = jnp.where(here, row * lax.rsqrt(pivot), scaled)
            row = row * inverse
            rows = jnp.where(here, row, rows - column * row)
            for k in range(8 if hi < n else 0):
                if k == p:
                    continue
                entry = row_of(columns[k], p)
                if k == p + 1:
                    kept = jnp.where(here, 0.0, columns[k])
                    columns[k] = kept - jnp.where(here, -entry, column * entry) * inverse
                else:
                    columns[k] = jnp.where(here, entry * inverse, columns[k] - column * (entry * inverse))
                under[k] = under[k] - under[p] * (entry * inverse)
            if hi < n:
                columns[p] = jnp.where(here, inverse, -column * inverse)
                under[p] = -under[p] * inverse
            else:
                for k in range(p + 1, 8):
                    entry = row_of(columns[k], p) * inverse
                    columns[k] = jnp.where(here, entry, columns[k] - column * entry)
        result[lo:hi, :] = jnp.where(lane <= sub + lo, scaled, 0.0)
        if hi < n:
            columns = [
                later[k] + total([under[p] * row_of(across[k], p) for p in range(8)])
                for k in range(8)
            ]
            lane_rest = lax.broadcasted_iota(jnp.int32, rest.shape, 1)
            kept = jnp.where((lane_rest >= lo) & (lane_rest < hi), 0.0, rest)
            work[hi:, :] = kept - total(
                [factors[k] * jnp.broadcast_to(rows[k : k + 1, :], rest.shape) for k in range(8)]
            )


def sweep_kernel(
    sweeps, place_ref, mine_ref, other_ref, start_ref, block_ref, blocks, gram, gram_high, gram_low,
    ahead, work, factor,
):
    place = place_ref[0]
    part = mine_ref.shape[0] // 4
    for k in range(4):
        quarter = ((place >> 2) & 3) ^ k
        mine = pl.multiple_of(((place & 1) * 4 + quarter) * part, 8)
        theirs = pl.multiple_of(((1 - (place & 1)) * 4 + quarter) * part, 8)
        blocks[pl.ds(mine, part), :] = mine_ref[k * part : (k + 1) * part, :]
        blocks[pl.ds(theirs, part), :] = other_ref[k * part : (k + 1) * part, :]
    n = gram.shape[0]
    above = upper_blocks(n)
    for number, (i, j) in enumerate(above):
        block = blocks[span(number), :]
        gram[span(i), span(j)] = block
        gram[span(j), span(i)] = block.T
    row, column = block_indices()
    tail = len(above) + n // EDGE // 2
    for pair in range(n // EDGE // 2):
        block = blocks[span(len(above) + pair), :]
        turned = block.T
        first, second = span(2 * pair), span(2 * pair + 1)
        diagonal = blocks[tail * EDGE + pair : tail * EDGE + pair + 1, :]
        gram[first, first] = jnp.where(row <= column, block, turned)
        gram[second, second] = jnp.where(
            row == column, diagonal, jnp.where(row > column, block, turned)
        )
    gram_high[...], gram_low[...] = halves(gram[...])

    def by_gram(block):
        high, low = halves(block)
        both = dot(jnp.concatenate([high, low], axis=0), gram_high[...], NN)
        rank = block.shape[0]
        return both[:rank] + both[rank:] + dot(high, gram_low[...], NN)

    block_ref[...] = by_gram(start_ref[...].T)

    def sweep(_, carry):
        block = block_ref[...]
        work[...] = dot(block, block, NT, HIGHEST)
        ahead[...] = by_gram(block)
        invert_factor(work, factor)
        block_ref[...] = split_dot(factor[...], ahead[...])
        return carry

    lax.fori_loop(0, sweeps - 1, sweep, 0)


def iterate(place, mine, other, start):
    n, rank = start.shape
    vmem = pl.BlockSpec(memory_space=pltpu.VMEM)
    return pl.pallas_call(
        functools.partial(sweep_kernel, SWEEPS),
        in_specs=[pl.BlockSpec(memory_space=pltpu.SMEM), vmem, vmem, vmem],
        out_specs=vmem,
        out_shape=jax.ShapeDtypeStruct((rank, n), jnp.float32),
        scratch_shapes=[
            pltpu.VMEM((2 * mine.shape[0], 128), jnp.float32),
            pltpu.VMEM((n, n), jnp.float32),
            pltpu.VMEM((n, n), jnp.bfloat16),
            pltpu.VMEM((n, n), jnp.bfloat16),
            pltpu.VMEM((rank, n), jnp.float32),
            pltpu.VMEM((rank, rank), jnp.float32),
            pltpu.VMEM((rank, rank), jnp.float32),
        ],
        cost_estimate=BRIEF,
        compiler_params=pltpu.CompilerParams(vmem_limit_bytes=16 * MIB),
        name="iterate",
    )(place, mine, other, start)


def factor_kernel(block_ref, out_ref, work):
    block = block_ref[...]
    work[...] = dot(block, block, NT, HIGHEST)
    invert_factor(work, out_ref)


def last_factor(block):
    rank = block.shape[0]
    vmem = pl.BlockSpec(memory_space=pltpu.VMEM)
    return pl.pallas_call(
        factor_kernel,
        in_specs=[vmem],
        out_specs=vmem,
        out_shape=jax.ShapeDtypeStruct((rank, rank), jnp.float32),
        scratch_shapes=[pltpu.VMEM((rank, rank), jnp.float32)],
        cost_estimate=BRIEF,
        compiler_params=pltpu.CompilerParams(vmem_limit_bytes=16 * MIB),
        name="last_factor",
    )(block)


def weights(block_ref):
    return jnp.concatenate(halves(block_ref[...]), axis=0)


def split_product(high, low, both):
    rank = both.shape[0] // 2
    product = dot(high, both, NT)
    return product[:, :rank] + product[:, rank:] + dot(low, both[:rank], NT)


def halved_product(x, both):
    return split_product(*halves(x), both)


def pick(held, place_ref, rank, first, fibres, j):
    start = first * 8 + (place_ref[1] ^ rank) * (8 // SLABS) + j
    return side_by_side(held, pl.ds(start, fibres, stride=8))


def chunks_of(rank):
    return sum(count for to, _, count in EARLY if to == rank)


def prepare_kernel(place_ref, held, *refs):
    per = 8 // SLABS
    high_ref, low_ref = refs[-2:]
    chunk = held.shape[1] // 8 // CHUNKS
    for (rank, first, count), out in zip(EARLY, refs[:-2], strict=True):
        for j in range(per):
            rows = pick(held, place_ref, rank, first * chunk, count * chunk, j)
            for c in range(out.shape[0]):
                out[c, pl.ds(j, count * chunk, stride=per), :] = rows[:, c * 128 : (c + 1) * 128]
    begin = 0
    for rank in (1, *FAR):
        first = chunks_of(rank) * chunk
        fibres = CHUNKS * chunk - first
        for j in range(per):
            high, low = halves(pick(held, place_ref, rank, first, fibres, j))
            high_ref[begin : begin + fibres, :] = high
            low_ref[begin : begin + fibres, :] = low
            begin += fibres


def prepare(place, held):
    columns, rows, lanes = held.shape
    chunk = rows // SLABS // CHUNKS
    count = sum(CHUNKS - chunks_of(rank) for rank in (1, *FAR)) * chunk
    split = jax.ShapeDtypeStruct((count, columns * lanes), jnp.bfloat16)
    sent = [
        jax.ShapeDtypeStruct((columns, some * chunk, lanes), jnp.float32) for _, _, some in EARLY
    ]
    vmem = pl.BlockSpec(memory_space=pltpu.VMEM)
    return pl.pallas_call(
        prepare_kernel,
        in_specs=[pl.BlockSpec(memory_space=pltpu.SMEM), vmem],
        out_specs=[vmem] * (len(sent) + 2),
        out_shape=[*sent, split, split],
        cost_estimate=BRIEF,
        compiler_params=pltpu.CompilerParams(vmem_limit_bytes=16 * MIB),
        name="prepare",
    )(place, held)


def sent_kernel(begin, groups, high_ref, low_ref, block_ref, *outs):
    per = 8 // SLABS
    both = weights(block_ref)
    outs = list(outs)
    for parts in groups:
        some = [outs.pop(0) for _ in range(parts)]
        fibres = sum(out.shape[0] for out in some) // per
        rows = slice(begin, begin + fibres * per)
        product = split_product(high_ref[rows, :], low_ref[rows, :], both)
        first = 0
        for out in some:
            count = out.shape[0] // per
            for j in range(per):
                start = j * fibres + first
                out[pl.ds(j, count, stride=per), :] = product[start : start + count]
            first += count
        begin += fibres * per


def project_sent(high, low, block, begin, groups, name):
    rank = block.shape[0]
    sizes = [size for group in groups for size in group]
    vmem = pl.BlockSpec(memory_space=pltpu.VMEM)
    return pl.pallas_call(
        functools.partial(sent_kernel, begin, [len(group) for group in groups]),
        in_specs=[vmem] * 3,
        out_specs=[vmem] * len(sizes),
        out_shape=[jax.ShapeDtypeStruct((size, rank), jnp.float32) for size in sizes],
        cost_estimate=BRIEF,
        compiler_params=pltpu.CompilerParams(vmem_limit_bytes=16 * MIB),
        name=name,
    )(high, low, block)


def own_kernel(place_ref, held, block_ref, out):
    per = 8 // SLABS
    both = weights(block_ref)
    fibres = held.shape[1] // 8
    x = jnp.concatenate([pick(held, place_ref, 0, 0, fibres, j) for j in range(per)], axis=0)
    product = halved_product(x, both)
    for j in range(per):
        out[pl.ds(j, fibres, stride=per), :] = product[j * fibres : (j + 1) * fibres]


def project_own(place, held, block):
    vmem = pl.BlockSpec(memory_space=pltpu.VMEM)
    return pl.pallas_call(
        own_kernel,
        in_specs=[pl.BlockSpec(memory_space=pltpu.SMEM), vmem, vmem],
        out_specs=vmem,
        out_shape=jax.ShapeDtypeStruct((held.shape[1] // SLABS, block.shape[0]), jnp.float32),
        cost_estimate=BRIEF,
        compiler_params=pltpu.CompilerParams(vmem_limit_bytes=16 * MIB),
        name="project_own",
    )(place, held, block)


def arrived_kernel(block_ref, *refs):
    outs = refs[-len(FAR) :]
    both = weights(block_ref)
    begins = [0] * len(FAR)
    for (rank, _, _), x_ref in zip(EARLY, refs[: len(EARLY)], strict=True):
        k, size = FAR.index(rank), x_ref.shape[1]
        x = side_by_side(x_ref, slice(None))
        outs[k][begins[k] : begins[k] + size, :] = halved_product(x, both)
        begins[k] += size


def project_arrived(block, arrived):
    vmem = pl.BlockSpec(memory_space=pltpu.VMEM)
    chunk = arrived[0].shape[1] // EARLY[0][2]
    return pl.pallas_call(
        arrived_kernel,
        in_specs=[vmem] * (1 + len(arrived)),
        out_specs=[vmem] * len(FAR),
        out_shape=[
            jax.ShapeDtypeStruct((chunks_of(rank) * chunk, block.shape[0]), jnp.float32)
            for rank in FAR
        ],
        cost_estimate=BRIEF,
        compiler_params=pltpu.CompilerParams(vmem_limit_bytes=16 * MIB),
        name="project_arrived",
    )(block, *arrived)


def finish_kernel(ranks, firsts, place_ref, factor_ref, *refs):
    pieces = refs[: len(ranks)]
    out, *results, sems = refs[-2 - len(ranks) :]
    factor = factor_ref[...]
    per, size = out.shape[2], out.shape[3]
    sends = []
    for k, (rank, first, piece) in enumerate(zip(ranks, firsts, pieces, strict=True)):
        last = first + results[k].shape[0]
        begin = first
        while begin < last:
            length = min(per - begin % per, last - begin)
            done = pl.ds(begin - first, length)
            rows = piece[(begin - first) * size : (begin - first + length) * size, :]
            results[k][done] = dot(rows, factor, NT, HIGHEST).reshape(length, size, -1)
            send = pltpu.make_async_copy(
                results[k].at[done],
                out.at[begin // per, place_ref[1] ^ rank, pl.ds(begin % per, length)],
                sems.at[k, begin // per],
            )
            send.start()
            sends.append(send)
            begin += length
    for send in sends:
        send.wait()


def finish(place, factor, pieces, ranks, firsts, into, name):
    shape = into if isinstance(into, tuple) else into.shape
    size, rank = shape[3:]
    vmem = pl.BlockSpec(memory_space=pltpu.VMEM)
    in_specs = [pl.BlockSpec(memory_space=pltpu.SMEM)] + [vmem] * (1 + len(pieces))
    operands = [place, factor, *pieces]
    aliases = {}
    if not isinstance(into, tuple):
        aliases = {len(operands): 0}
        in_specs.append(pl.BlockSpec(memory_space=pl.ANY))
        operands.append(into)
    return pl.pallas_call(
        functools.partial(finish_kernel, ranks, firsts),
        in_specs=in_specs,
        out_specs=pl.BlockSpec(memory_space=pl.ANY),
        out_shape=jax.ShapeDtypeStruct(shape, jnp.float32),
        scratch_shapes=[
            pltpu.VMEM((piece.shape[0] // size, size, rank), jnp.float32) for piece in pieces
        ]
        + [pltpu.SemaphoreType.DMA((len(pieces), shape[0]))],
        input_output_aliases=aliases,
        cost_estimate=BRIEF,
        compiler_params=pltpu.CompilerParams(vmem_limit_bytes=16 * MIB),
        name=name,
    )(*operands)


def per_device(fields, start_basis):
    nv, n2, n3, n1 = fields.shape
    slabs = lax.axis_size("slab")
    slab = lax.axis_index("slab")
    place = jnp.stack([lax.axis_index("wide") * slabs + slab, slab]).astype(jnp.int32)
    rows = fields.reshape(-1, n1)
    count = float(rows.shape[0] * lax.axis_size("wide") * slabs)
    def to_far(some, ranks):
        return [exchange(x, "slab", rank) for x, rank in zip(some, ranks, strict=True)]

    def send(prepared):
        *sent, high, low = prepared
        ranks = [rank for rank, _, _ in EARLY]
        return [high, low], to_far(sent, ranks)

    keep, give, held = local_gram(place, rows, count)
    prepared = prepare(place, held)
    mine, other, (high, low), arrived = sum_gram(keep, give, prepared, send)
    block = iterate(place, mine, other, start_basis)

    block, *arrived = lax.optimization_barrier((block, *arrived))
    chunk = rows.shape[0] // SLABS // CHUNKS
    near_rows = CHUNKS * chunk
    far_rows = [[(CHUNKS - chunks_of(rank)) * chunk] for rank in FAR]
    far = project_sent(high, low, block, near_rows, far_rows, "project_far")
    block, far = lax.optimization_barrier((block, far))
    far = to_far(far, FAR)
    near = project_sent(high, low, block, 0, [[near_rows // 2] * 2], "project_near")
    near = [exchange(x, "slab", 1) for x in near]
    own = project_own(place, held, block)
    arrived = project_arrived(block, arrived)
    factor = last_factor(block)

    per = CHUNKS // nv
    out = (nv, slabs, per, n2 * n3 // slabs // per, block.shape[0])
    late = [chunks_of(rank) for rank in FAR]
    out = finish(place, factor, arrived, FAR, (0, 0), out, "finish_arrived")
    out = finish(place, factor, far[:1], FAR[:1], late[:1], out, "finish_first_far")
    out = finish(place, factor, [own, *near], (0, 1, 1), (0, 0, CHUNKS // 2), out, "finish_near")
    out = finish(place, factor, far[1:], FAR[1:], late[1:], out, "finish_last_far")
    return out.reshape(nv, n2 * slabs, n3 // slabs, out.shape[-1])


def solution(mesh):
    in_specs = (P(None, "slab", "wide", None), P())
    out_specs = P(None, None, ("wide", "slab"), None)
    return jax.shard_map(
        per_device, mesh=mesh, in_specs=in_specs, out_specs=out_specs, check_vma=False
    )
```

```python
import functools

import jax
import jax.numpy as jnp
from jax import lax
from jax.experimental import pallas as pl
from jax.experimental.pallas import tpu as pltpu
from jax.sharding import PartitionSpec as P

SWEEPS = 4
SLABS = 4
CHUNKS = 16
EARLY = ((2, 0, 4), (3, 0, 4))
FAR = (2, 3)
TILES = (1, 1, 2, 2, 2)
AXES = ("wide", "slab")
MIB = 1 << 20
HIGHEST = lax.Precision.HIGHEST
NN = (((1,), (0,)), ((), ()))
NT = (((1,), (1,)), ((), ()))
TN = (((0,), (0,)), ((), ()))
BRIEF = pl.CostEstimate(flops=1, bytes_accessed=1, transcendentals=0)


def dot(a, b, dims, precision=None):
    return lax.dot_general(a, b, dims, precision=precision, preferred_element_type=jnp.float32)


def halves(x):
    high = x.astype(jnp.bfloat16)
    return high, (x - high.astype(jnp.float32)).astype(jnp.bfloat16)


def thirds(x):
    high = x.astype(jnp.bfloat16)
    middle, low = halves(x - high.astype(jnp.float32))
    return high, middle, low


def exchange(value, axes, mask):
    size = 1
    for axis in axes if isinstance(axes, tuple) else (axes,):
        size *= lax.axis_size(axis)
    return lax.ppermute(value, axes, [(i, i ^ mask) for i in range(size)])


EDGE = 128


def upper_blocks(n):
    return [(i, j) for i in range(n // EDGE) for j in range(i + 1, n // EDGE)]


def packed_rows(n):
    return pl.cdiv((len(upper_blocks(n)) + n // EDGE // 2) * EDGE + 8, 64) * 64


def span(number):
    return slice(number * EDGE, (number + 1) * EDGE)


def block_indices():
    return [lax.broadcasted_iota(jnp.int32, (EDGE, EDGE), axis) for axis in (0, 1)]


def copies(x_ref, held, sems):
    tile = held.shape[1] // sems.shape[0]
    return [
        [
            pltpu.make_async_copy(
                x_ref.at[pl.ds(i * tile, tile), pl.ds(c * 128, 128)],
                held.at[c, pl.ds(i * tile, tile)],
                sems.at[i, c],
            )
            for c in range(held.shape[0])
        ]
        for i in range(sems.shape[0])
    ]


def side_by_side(ref, rows):
    return jnp.concatenate([ref[c, rows, :] for c in range(ref.shape[0])], axis=1)


def gram_kernel(scale, place_ref, x_ref, *refs):
    keep_ref, give_ref, held, acc, whole, sems = refs
    n = held.shape[0] * held.shape[2]
    half = n // 2
    arrivals = copies(x_ref, held, sems)
    for arrival in arrivals:
        for copy in arrival:
            copy.start()
    tile = held.shape[1] // len(arrivals)
    first = 0
    for count in TILES:
        for arrival in arrivals[first : first + count]:
            for copy in arrival:
                copy.wait()
        high, low = halves(side_by_side(held, pl.ds(first * tile, count * tile)))
        left = dot(high[:, :half], jnp.concatenate([high, low], axis=1), TN)
        right = dot(high[:, half:], jnp.concatenate([high[:, half:], low], axis=1), TN)
        if first == 0:
            acc[:half, :] = left
            acc[half:, half:] = right
        else:
            acc[:half, :] += left
            acc[half:, half:] += right
        first += count

    def block(i, j):
        cross = acc[span(i), n + j * EDGE : n + (j + 1) * EDGE]
        other = acc[span(j), n + i * EDGE : n + (i + 1) * EDGE]
        return (acc[span(i), span(j)] + cross + other.T) * scale

    above = upper_blocks(n)
    for number, (i, j) in enumerate(above):
        whole[span(number), :] = block(i, j)
    row, column = block_indices()
    tail = len(above) + n // EDGE // 2
    whole[tail * EDGE :, :] = jnp.zeros((whole.shape[0] - tail * EDGE, EDGE), jnp.float32)
    for pair in range(n // EDGE // 2):
        first, second = block(2 * pair, 2 * pair), block(2 * pair + 1, 2 * pair + 1)
        whole[span(len(above) + pair), :] = jnp.where(row <= column, first, second)
        diagonal = jnp.sum(jnp.where(row == column, second, 0.0), axis=0, keepdims=True)
        whole[tail * EDGE + pair : tail * EDGE + pair + 1, :] = diagonal
    place = place_ref[0]
    part = keep_ref.shape[0] // 4
    for k in range(4):
        quarter = ((place >> 2) & 3) ^ k
        mine = pl.multiple_of(((place & 1) * 4 + quarter) * part, 8)
        theirs = pl.multiple_of(((1 - (place & 1)) * 4 + quarter) * part, 8)
        keep_ref[k * part : (k + 1) * part, :] = whole[pl.ds(mine, part), :]
        give_ref[k * part : (k + 1) * part, :] = whole[pl.ds(theirs, part), :]


def local_gram(place, rows, count):
    n = rows.shape[1]
    tall = packed_rows(n)
    half = jax.ShapeDtypeStruct((tall // 2, 128), jnp.float32)
    held = jax.ShapeDtypeStruct((n // 128, rows.shape[0], 128), jnp.float32)
    vmem = pl.BlockSpec(memory_space=pltpu.VMEM)
    return pl.pallas_call(
        functools.partial(gram_kernel, 1.0 / count),
        in_specs=[pl.BlockSpec(memory_space=pltpu.SMEM), pl.BlockSpec(memory_space=pl.ANY)],
        out_specs=[vmem] * 3,
        out_shape=[half, half, held],
        scratch_shapes=[
            pltpu.VMEM((n, 2 * n), jnp.float32),
            pltpu.VMEM((tall, 128), jnp.float32),
            pltpu.SemaphoreType.DMA((sum(TILES), n // 128)),
        ],
        cost_estimate=BRIEF,
        compiler_params=pltpu.CompilerParams(vmem_limit_bytes=40 * MIB),
        name="local_gram",
    )(place, rows)


def sum_gram(keep, give, prepared, send):
    size = lax.axis_size("wide") * lax.axis_size("slab")
    held = keep + exchange(give, AXES, 1)
    part = held.shape[0] // 4
    pieces = [held[k * part : (k + 1) * part] for k in range(4)]
    total = pieces[0]
    arrived = [exchange(pieces[k], AXES, 4 * k) for k in range(1, 4)]
    for piece in arrived:
        total = total + piece
    total = total + exchange(total, AXES, 2)
    total, prepared = lax.optimization_barrier((total, prepared))
    soon, more = send(prepared)
    mask = 16
    while mask < size:
        total = total + exchange(total, AXES, mask)
        mask *= 2
    mine = jnp.concatenate([total] + [exchange(total, AXES, 4 * k) for k in range(1, 4)])
    mine, soon = lax.optimization_barrier((mine, soon))
    return mine, exchange(mine, AXES, 1), soon, more


def row_of(x, p):
    return jnp.broadcast_to(x[p : p + 1, :], x.shape)


def column_of(x, k):
    return jnp.broadcast_to(x[:, k : k + 1], x.shape)


def total(terms):
    while len(terms) > 1:
        odd = terms[len(terms) & ~1 :]
        terms = [x + y for x, y in zip(terms[::2], terms[1::2], strict=False)] + odd
    return terms[0]


def invert_factor(work, result):
    n = work.shape[0]
    lane = lax.broadcasted_iota(jnp.int32, (8, n), 1)
    sub = lax.broadcasted_iota(jnp.int32, (8, n), 0)
    columns = [column_of(work[:8, :], k) for k in range(8)]
    for lo in range(0, n, 8):
        hi = lo + 8
        rows = work[lo:hi, :]
        if hi < n:
            rest = work[hi:, :]
            factors = [column_of(rest, lo + k) for k in range(8)]
            across = [column_of(rows, hi + k) for k in range(8)]
            later = [column_of(rest[:8], hi + k) for k in range(8)]
            under = [x[:8] for x in factors]
        rows = jnp.where((lane >= lo) & (lane < hi), (lane - lo == sub).astype(jnp.float32), rows)
        scaled = jnp.zeros((8, n), jnp.float32)
        for p in range(8):
            here = sub == p
            column = columns[p]
            pivot = row_of(column, p)
            inverse = 1.0 / pivot
            row = row_of(rows, p)
            scaled = jnp.where(here, row * lax.rsqrt(pivot), scaled)
            row = row * inverse
            rows = jnp.where(here, row, rows - column * row)
            for k in range(8 if hi < n else 0):
                if k == p:
                    continue
                entry = row_of(columns[k], p)
                if k == p + 1:
                    kept = jnp.where(here, 0.0, columns[k])
                    columns[k] = kept - jnp.where(here, -entry, column * entry) * inverse
                else:
                    columns[k] = jnp.where(here, entry * inverse, columns[k] - column * (entry * inverse))
                under[k] = under[k] - under[p] * (entry * inverse)
            if hi < n:
                columns[p] = jnp.where(here, inverse, -column * inverse)
                under[p] = -under[p] * inverse
            else:
                for k in range(p + 1, 8):
                    entry = row_of(columns[k], p) * inverse
                    columns[k] = jnp.where(here, entry, columns[k] - column * entry)
        result[lo:hi, :] = jnp.where(lane <= sub + lo, scaled, 0.0)
        if hi < n:
            columns = [
                later[k] + total([under[p] * row_of(across[k], p) for p in range(8)])
                for k in range(8)
            ]
            lane_rest = lax.broadcasted_iota(jnp.int32, rest.shape, 1)
            kept = jnp.where((lane_rest >= lo) & (lane_rest < hi), 0.0, rest)
            work[hi:, :] = kept - total(
                [factors[k] * jnp.broadcast_to(rows[k : k + 1, :], rest.shape) for k in range(8)]
            )


def sweep_kernel(
    sweeps, place_ref, mine_ref, other_ref, start_ref, block_ref, blocks, gram, gram_high, gram_middle, gram_low,
    ahead, work, factor,
):
    place = place_ref[0]
    part = mine_ref.shape[0] // 4
    for k in range(4):
        quarter = ((place >> 2) & 3) ^ k
        mine = pl.multiple_of(((place & 1) * 4 + quarter) * part, 8)
        theirs = pl.multiple_of(((1 - (place & 1)) * 4 + quarter) * part, 8)
        blocks[pl.ds(mine, part), :] = mine_ref[k * part : (k + 1) * part, :]
        blocks[pl.ds(theirs, part), :] = other_ref[k * part : (k + 1) * part, :]
    n = gram.shape[0]
    above = upper_blocks(n)
    for number, (i, j) in enumerate(above):
        block = blocks[span(number), :]
        gram[span(i), span(j)] = block
        gram[span(j), span(i)] = block.T
    row, column = block_indices()
    tail = len(above) + n // EDGE // 2
    for pair in range(n // EDGE // 2):
        block = blocks[span(len(above) + pair), :]
        turned = block.T
        first, second = span(2 * pair), span(2 * pair + 1)
        diagonal = blocks[tail * EDGE + pair : tail * EDGE + pair + 1, :]
        gram[first, first] = jnp.where(row <= column, block, turned)
        gram[second, second] = jnp.where(
            row == column, diagonal, jnp.where(row > column, block, turned)
        )
    gram_high[...], gram_middle[...], gram_low[...] = thirds(gram[...])

    def by_gram(block):
        rank = block.shape[0]
        parts = jnp.concatenate(thirds(block), axis=0)
        large = dot(parts, gram_high[...], NN)
        small = dot(parts[: 2 * rank], gram_middle[...], NN)
        least = dot(parts[:rank], gram_low[...], NN) + small[rank:] + large[2 * rank :]
        return large[:rank] + (large[rank : 2 * rank] + small[:rank] + least)

    block_ref[...] = by_gram(start_ref[...].T)

    def sweep(_, carry):
        block = block_ref[...]
        work[...] = dot(block, block, NT, HIGHEST)
        ahead[...] = by_gram(block)
        invert_factor(work, factor)
        block_ref[...] = dot(factor[...], ahead[...], NN, HIGHEST)
        return carry

    lax.fori_loop(0, sweeps - 1, sweep, 0)


def iterate(place, mine, other, start):
    n, rank = start.shape
    vmem = pl.BlockSpec(memory_space=pltpu.VMEM)
    return pl.pallas_call(
        functools.partial(sweep_kernel, SWEEPS),
        in_specs=[pl.BlockSpec(memory_space=pltpu.SMEM), vmem, vmem, vmem],
        out_specs=vmem,
        out_shape=jax.ShapeDtypeStruct((rank, n), jnp.float32),
        scratch_shapes=[
            pltpu.VMEM((2 * mine.shape[0], 128), jnp.float32),
            pltpu.VMEM((n, n), jnp.float32),
            pltpu.VMEM((n, n), jnp.bfloat16),
            pltpu.VMEM((n, n), jnp.bfloat16),
            pltpu.VMEM((n, n), jnp.bfloat16),
            pltpu.VMEM((rank, n), jnp.float32),
            pltpu.VMEM((rank, rank), jnp.float32),
            pltpu.VMEM((rank, rank), jnp.float32),
        ],
        cost_estimate=BRIEF,
        compiler_params=pltpu.CompilerParams(vmem_limit_bytes=16 * MIB),
        name="iterate",
    )(place, mine, other, start)


def factor_kernel(block_ref, out_ref, work):
    block = block_ref[...]
    work[...] = dot(block, block, NT, HIGHEST)
    invert_factor(work, out_ref)


def last_factor(block):
    rank = block.shape[0]
    vmem = pl.BlockSpec(memory_space=pltpu.VMEM)
    return pl.pallas_call(
        factor_kernel,
        in_specs=[vmem],
        out_specs=vmem,
        out_shape=jax.ShapeDtypeStruct((rank, rank), jnp.float32),
        scratch_shapes=[pltpu.VMEM((rank, rank), jnp.float32)],
        cost_estimate=BRIEF,
        compiler_params=pltpu.CompilerParams(vmem_limit_bytes=16 * MIB),
        name="last_factor",
    )(block)


def weights(block_ref):
    return jnp.concatenate(halves(block_ref[...]), axis=0)


def split_product(high, low, both):
    rank = both.shape[0] // 2
    product = dot(high, both, NT)
    return product[:, :rank] + product[:, rank:] + dot(low, both[:rank], NT)


def halved_product(x, both):
    return split_product(*halves(x), both)


def pick(held, place_ref, rank, first, fibres, j):
    start = first * 8 + (place_ref[1] ^ rank) * (8 // SLABS) + j
    return side_by_side(held, pl.ds(start, fibres, stride=8))


def chunks_of(rank):
    return sum(count for to, _, count in EARLY if to == rank)


def prepare_kernel(place_ref, held, *refs):
    per = 8 // SLABS
    high_ref, low_ref = refs[-2:]
    chunk = held.shape[1] // 8 // CHUNKS
    for (rank, first, count), out in zip(EARLY, refs[:-2], strict=True):
        for j in range(per):
            rows = pick(held, place_ref, rank, first * chunk, count * chunk, j)
            for c in range(out.shape[0]):
                out[c, pl.ds(j, count * chunk, stride=per), :] = rows[:, c * 128 : (c + 1) * 128]
    begin = 0
    for rank in (1, *FAR):
        first = chunks_of(rank) * chunk
        fibres = CHUNKS * chunk - first
        for j in range(per):
            high, low = halves(pick(held, place_ref, rank, first, fibres, j))
            high_ref[begin : begin + fibres, :] = high
            low_ref[begin : begin + fibres, :] = low
            begin += fibres


def prepare(place, held):
    columns, rows, lanes = held.shape
    chunk = rows // SLABS // CHUNKS
    count = sum(CHUNKS - chunks_of(rank) for rank in (1, *FAR)) * chunk
    split = jax.ShapeDtypeStruct((count, columns * lanes), jnp.bfloat16)
    sent = [
        jax.ShapeDtypeStruct((columns, some * chunk, lanes), jnp.float32) for _, _, some in EARLY
    ]
    vmem = pl.BlockSpec(memory_space=pltpu.VMEM)
    return pl.pallas_call(
        prepare_kernel,
        in_specs=[pl.BlockSpec(memory_space=pltpu.SMEM), vmem],
        out_specs=[vmem] * (len(sent) + 2),
        out_shape=[*sent, split, split],
        cost_estimate=BRIEF,
        compiler_params=pltpu.CompilerParams(vmem_limit_bytes=16 * MIB),
        name="prepare",
    )(place, held)


def sent_kernel(begin, groups, high_ref, low_ref, block_ref, *outs):
    per = 8 // SLABS
    both = weights(block_ref)
    outs = list(outs)
    for parts in groups:
        some = [outs.pop(0) for _ in range(parts)]
        fibres = sum(out.shape[0] for out in some) // per
        rows = slice(begin, begin + fibres * per)
        product = split_product(high_ref[rows, :], low_ref[rows, :], both)
        first = 0
        for out in some:
            count = out.shape[0] // per
            for j in range(per):
                start = j * fibres + first
                out[pl.ds(j, count, stride=per), :] = product[start : start + count]
            first += count
        begin += fibres * per


def project_sent(high, low, block, begin, groups, name):
    rank = block.shape[0]
    sizes = [size for group in groups for size in group]
    vmem = pl.BlockSpec(memory_space=pltpu.VMEM)
    return pl.pallas_call(
        functools.partial(sent_kernel, begin, [len(group) for group in groups]),
        in_specs=[vmem] * 3,
        out_specs=[vmem] * len(sizes),
        out_shape=[jax.ShapeDtypeStruct((size, rank), jnp.float32) for size in sizes],
        cost_estimate=BRIEF,
        compiler_params=pltpu.CompilerParams(vmem_limit_bytes=16 * MIB),
        name=name,
    )(high, low, block)


def own_kernel(place_ref, held, block_ref, out):
    per = 8 // SLABS
    both = weights(block_ref)
    fibres = held.shape[1] // 8
    x = jnp.concatenate([pick(held, place_ref, 0, 0, fibres, j) for j in range(per)], axis=0)
    product = halved_product(x, both)
    for j in range(per):
        out[pl.ds(j, fibres, stride=per), :] = product[j * fibres : (j + 1) * fibres]


def project_own(place, held, block):
    vmem = pl.BlockSpec(memory_space=pltpu.VMEM)
    return pl.pallas_call(
        own_kernel,
        in_specs=[pl.BlockSpec(memory_space=pltpu.SMEM), vmem, vmem],
        out_specs=vmem,
        out_shape=jax.ShapeDtypeStruct((held.shape[1] // SLABS, block.shape[0]), jnp.float32),
        cost_estimate=BRIEF,
        compiler_params=pltpu.CompilerParams(vmem_limit_bytes=16 * MIB),
        name="project_own",
    )(place, held, block)


def arrived_kernel(block_ref, *refs):
    outs = refs[-len(FAR) :]
    both = weights(block_ref)
    begins = [0] * len(FAR)
    for (rank, _, _), x_ref in zip(EARLY, refs[: len(EARLY)], strict=True):
        k, size = FAR.index(rank), x_ref.shape[1]
        x = side_by_side(x_ref, slice(None))
        outs[k][begins[k] : begins[k] + size, :] = halved_product(x, both)
        begins[k] += size


def project_arrived(block, arrived):
    vmem = pl.BlockSpec(memory_space=pltpu.VMEM)
    chunk = arrived[0].shape[1] // EARLY[0][2]
    return pl.pallas_call(
        arrived_kernel,
        in_specs=[vmem] * (1 + len(arrived)),
        out_specs=[vmem] * len(FAR),
        out_shape=[
            jax.ShapeDtypeStruct((chunks_of(rank) * chunk, block.shape[0]), jnp.float32)
            for rank in FAR
        ],
        cost_estimate=BRIEF,
        compiler_params=pltpu.CompilerParams(vmem_limit_bytes=16 * MIB),
        name="project_arrived",
    )(block, *arrived)


def finish_kernel(ranks, firsts, place_ref, factor_ref, *refs):
    pieces = refs[: len(ranks)]
    out, *results, sems = refs[-2 - len(ranks) :]
    factor = factor_ref[...]
    per, size = out.shape[2], out.shape[3]
    sends = []
    for k, (rank, first, piece) in enumerate(zip(ranks, firsts, pieces, strict=True)):
        last = first + results[k].shape[0]
        begin = first
        while begin < last:
            length = min(per - begin % per, last - begin)
            done = pl.ds(begin - first, length)
            rows = piece[(begin - first) * size : (begin - first + length) * size, :]
            results[k][done] = dot(rows, factor, NT, HIGHEST).reshape(length, size, -1)
            send = pltpu.make_async_copy(
                results[k].at[done],
                out.at[begin // per, place_ref[1] ^ rank, pl.ds(begin % per, length)],
                sems.at[k, begin // per],
            )
            send.start()
            sends.append(send)
            begin += length
    for send in sends:
        send.wait()


def finish(place, factor, pieces, ranks, firsts, into, name):
    shape = into if isinstance(into, tuple) else into.shape
    size, rank = shape[3:]
    vmem = pl.BlockSpec(memory_space=pltpu.VMEM)
    in_specs = [pl.BlockSpec(memory_space=pltpu.SMEM)] + [vmem] * (1 + len(pieces))
    operands = [place, factor, *pieces]
    aliases = {}
    if not isinstance(into, tuple):
        aliases = {len(operands): 0}
        in_specs.append(pl.BlockSpec(memory_space=pl.ANY))
        operands.append(into)
    return pl.pallas_call(
        functools.partial(finish_kernel, ranks, firsts),
        in_specs=in_specs,
        out_specs=pl.BlockSpec(memory_space=pl.ANY),
        out_shape=jax.ShapeDtypeStruct(shape, jnp.float32),
        scratch_shapes=[
            pltpu.VMEM((piece.shape[0] // size, size, rank), jnp.float32) for piece in pieces
        ]
        + [pltpu.SemaphoreType.DMA((len(pieces), shape[0]))],
        input_output_aliases=aliases,
        cost_estimate=BRIEF,
        compiler_params=pltpu.CompilerParams(vmem_limit_bytes=16 * MIB),
        name=name,
    )(*operands)


def per_device(fields, start_basis):
    nv, n2, n3, n1 = fields.shape
    slabs = lax.axis_size("slab")
    slab = lax.axis_index("slab")
    place = jnp.stack([lax.axis_index("wide") * slabs + slab, slab]).astype(jnp.int32)
    rows = fields.reshape(-1, n1)
    count = float(rows.shape[0] * lax.axis_size("wide") * slabs)
    def to_far(some, ranks):
        return [exchange(x, "slab", rank) for x, rank in zip(some, ranks, strict=True)]

    def send(prepared):
        *sent, high, low = prepared
        ranks = [rank for rank, _, _ in EARLY]
        return [high, low], to_far(sent, ranks)

    keep, give, held = local_gram(place, rows, count)
    prepared = prepare(place, held)
    mine, other, (high, low), arrived = sum_gram(keep, give, prepared, send)
    block = iterate(place, mine, other, start_basis)

    block, *arrived = lax.optimization_barrier((block, *arrived))
    chunk = rows.shape[0] // SLABS // CHUNKS
    near_rows = CHUNKS * chunk
    far_rows = [[(CHUNKS - chunks_of(rank)) * chunk] for rank in FAR]
    far = project_sent(high, low, block, near_rows, far_rows, "project_far")
    block, far = lax.optimization_barrier((block, far))
    far = to_far(far, FAR)
    near = project_sent(high, low, block, 0, [[near_rows // 2] * 2], "project_near")
    near = [exchange(x, "slab", 1) for x in near]
    own = project_own(place, held, block)
    arrived = project_arrived(block, arrived)
    factor = last_factor(block)

    per = CHUNKS // nv
    out = (nv, slabs, per, n2 * n3 // slabs // per, block.shape[0])
    late = [chunks_of(rank) for rank in FAR]
    out = finish(place, factor, arrived, FAR, (0, 0), out, "finish_arrived")
    out = finish(place, factor, far[:1], FAR[:1], late[:1], out, "finish_first_far")
    out = finish(place, factor, [own, *near], (0, 1, 1), (0, 0, CHUNKS // 2), out, "finish_near")
    out = finish(place, factor, far[1:], FAR[1:], late[1:], out, "finish_last_far")
    return out.reshape(nv, n2 * slabs, n3 // slabs, out.shape[-1])


def solution(mesh):
    in_specs = (P(None, "slab", "wide", None), P())
    out_specs = P(None, None, ("wide", "slab"), None)
    return jax.shard_map(
        per_device, mesh=mesh, in_specs=in_specs, out_specs=out_specs, check_vma=False
    )
```

```python
import functools

import jax
import jax.numpy as jnp
from jax import lax
from jax.experimental import pallas as pl
from jax.experimental.pallas import tpu as pltpu
from jax.sharding import PartitionSpec as P

SWEEPS = 4
SLABS = 4
CHUNKS = 16
EARLY = ((2, 0, 4), (3, 0, 4))
FAR = (2, 3)
TILES = (1, 1, 2, 2, 2)
AXES = ("wide", "slab")
MIB = 1 << 20
HIGHEST = lax.Precision.HIGHEST
NN = (((1,), (0,)), ((), ()))
NT = (((1,), (1,)), ((), ()))
TN = (((0,), (0,)), ((), ()))
BRIEF = pl.CostEstimate(flops=1, bytes_accessed=1, transcendentals=0)


def dot(a, b, dims, precision=None):
    return lax.dot_general(a, b, dims, precision=precision, preferred_element_type=jnp.float32)


def halves(x):
    high = x.astype(jnp.bfloat16)
    return high, (x - high.astype(jnp.float32)).astype(jnp.bfloat16)


def split_dot(a, b):
    a_high, a_low = halves(a)
    b_high, b_low = halves(b)
    both = dot(jnp.concatenate([a_high, a_low], axis=0), b_high, NN)
    rows = a.shape[0]
    return both[:rows] + both[rows:] + dot(a_high, b_low, NN)


def exchange(value, axes, mask):
    size = 1
    for axis in axes if isinstance(axes, tuple) else (axes,):
        size *= lax.axis_size(axis)
    return lax.ppermute(value, axes, [(i, i ^ mask) for i in range(size)])


EDGE = 128


def upper_blocks(n):
    return [(i, j) for i in range(n // EDGE) for j in range(i + 1, n // EDGE)]


def packed_rows(n):
    return pl.cdiv((len(upper_blocks(n)) + n // EDGE // 2) * EDGE + 8, 64) * 64


def span(number):
    return slice(number * EDGE, (number + 1) * EDGE)


def block_indices():
    return [lax.broadcasted_iota(jnp.int32, (EDGE, EDGE), axis) for axis in (0, 1)]


def copies(x_ref, held, sems):
    tile = held.shape[1] // sems.shape[0]
    return [
        [
            pltpu.make_async_copy(
                x_ref.at[pl.ds(i * tile, tile), pl.ds(c * 128, 128)],
                held.at[c, pl.ds(i * tile, tile)],
                sems.at[i, c],
            )
            for c in range(held.shape[0])
        ]
        for i in range(sems.shape[0])
    ]


def side_by_side(ref, rows):
    return jnp.concatenate([ref[c, rows, :] for c in range(ref.shape[0])], axis=1)


def gram_kernel(scale, place_ref, x_ref, *refs):
    keep_ref, give_ref, held, acc, whole, sems = refs
    n = held.shape[0] * held.shape[2]
    half = n // 2
    arrivals = copies(x_ref, held, sems)
    for arrival in arrivals:
        for copy in arrival:
            copy.start()
    tile = held.shape[1] // len(arrivals)
    first = 0
    for count in TILES:
        for arrival in arrivals[first : first + count]:
            for copy in arrival:
                copy.wait()
        high, low = halves(side_by_side(held, pl.ds(first * tile, count * tile)))
        left = dot(high[:, :half], jnp.concatenate([high, low], axis=1), TN)
        right = dot(high[:, half:], jnp.concatenate([high[:, half:], low], axis=1), TN)
        if first == 0:
            acc[:half, :] = left
            acc[half:, half:] = right
        else:
            acc[:half, :] += left
            acc[half:, half:] += right
        first += count

    def block(i, j):
        cross = acc[span(i), n + j * EDGE : n + (j + 1) * EDGE]
        other = acc[span(j), n + i * EDGE : n + (i + 1) * EDGE]
        return (acc[span(i), span(j)] + cross + other.T) * scale

    above = upper_blocks(n)
    for number, (i, j) in enumerate(above):
        whole[span(number), :] = block(i, j)
    row, column = block_indices()
    tail = len(above) + n // EDGE // 2
    whole[tail * EDGE :, :] = jnp.zeros((whole.shape[0] - tail * EDGE, EDGE), jnp.float32)
    for pair in range(n // EDGE // 2):
        first, second = block(2 * pair, 2 * pair), block(2 * pair + 1, 2 * pair + 1)
        whole[span(len(above) + pair), :] = jnp.where(row <= column, first, second)
        diagonal = jnp.sum(jnp.where(row == column, second, 0.0), axis=0, keepdims=True)
        whole[tail * EDGE + pair : tail * EDGE + pair + 1, :] = diagonal
    place = place_ref[0]
    part = keep_ref.shape[0] // 4
    for k in range(4):
        quarter = ((place >> 2) & 3) ^ k
        mine = pl.multiple_of(((place & 1) * 4 + quarter) * part, 8)
        theirs = pl.multiple_of(((1 - (place & 1)) * 4 + quarter) * part, 8)
        keep_ref[k * part : (k + 1) * part, :] = whole[pl.ds(mine, part), :]
        give_ref[k * part : (k + 1) * part, :] = whole[pl.ds(theirs, part), :]


def local_gram(place, rows, count):
    n = rows.shape[1]
    tall = packed_rows(n)
    half = jax.ShapeDtypeStruct((tall // 2, 128), jnp.float32)
    held = jax.ShapeDtypeStruct((n // 128, rows.shape[0], 128), jnp.float32)
    vmem = pl.BlockSpec(memory_space=pltpu.VMEM)
    return pl.pallas_call(
        functools.partial(gram_kernel, 1.0 / count),
        in_specs=[pl.BlockSpec(memory_space=pltpu.SMEM), pl.BlockSpec(memory_space=pl.ANY)],
        out_specs=[vmem] * 3,
        out_shape=[half, half, held],
        scratch_shapes=[
            pltpu.VMEM((n, 2 * n), jnp.float32),
            pltpu.VMEM((tall, 128), jnp.float32),
            pltpu.SemaphoreType.DMA((sum(TILES), n // 128)),
        ],
        cost_estimate=BRIEF,
        compiler_params=pltpu.CompilerParams(vmem_limit_bytes=40 * MIB),
        name="local_gram",
    )(place, rows)


def sum_gram(keep, give, prepared, send):
    size = lax.axis_size("wide") * lax.axis_size("slab")
    held = keep + exchange(give, AXES, 1)
    part = held.shape[0] // 4
    pieces = [held[k * part : (k + 1) * part] for k in range(4)]
    total = pieces[0]
    arrived = [exchange(pieces[k], AXES, 4 * k) for k in range(1, 4)]
    for piece in arrived:
        total = total + piece
    total = total + exchange(total, AXES, 2)
    total, prepared = lax.optimization_barrier((total, prepared))
    soon, more = send(prepared)
    mask = 16
    while mask < size:
        total = total + exchange(total, AXES, mask)
        mask *= 2
    mine = jnp.concatenate([total] + [exchange(total, AXES, 4 * k) for k in range(1, 4)])
    mine, soon = lax.optimization_barrier((mine, soon))
    return mine, exchange(mine, AXES, 1), soon, more


def row_of(x, p):
    return jnp.broadcast_to(x[p : p + 1, :], x.shape)


def column_of(x, k):
    return jnp.broadcast_to(x[:, k : k + 1], x.shape)


def total(terms):
    while len(terms) > 1:
        odd = terms[len(terms) & ~1 :]
        terms = [x + y for x, y in zip(terms[::2], terms[1::2], strict=False)] + odd
    return terms[0]


def invert_factor(work, result):
    n = work.shape[0]
    lane = lax.broadcasted_iota(jnp.int32, (8, n), 1)
    sub = lax.broadcasted_iota(jnp.int32, (8, n), 0)
    columns = [column_of(work[:8, :], k) for k in range(8)]
    for lo in range(0, n, 8):
        hi = lo + 8
        rows = work[lo:hi, :]
        if hi < n:
            rest = work[hi:, :]
            factors = [column_of(rest, lo + k) for k in range(8)]
            across = [column_of(rows, hi + k) for k in range(8)]
            later = [column_of(rest[:8], hi + k) for k in range(8)]
            under = [x[:8] for x in factors]
        rows = jnp.where((lane >= lo) & (lane < hi), (lane - lo == sub).astype(jnp.float32), rows)
        scaled = jnp.zeros((8, n), jnp.float32)
        for p in range(8):
            here = sub == p
            column = columns[p]
            pivot = row_of(column, p)
            inverse = 1.0 / pivot
            row = row_of(rows, p)
            scaled = jnp.where(here, row * lax.rsqrt(pivot), scaled)
            row = row * inverse
            rows = jnp.where(here, row, rows - column * row)
            for k in range(8 if hi < n else 0):
                if k == p:
                    continue
                entry = row_of(columns[k], p)
                if k == p + 1:
                    kept = jnp.where(here, 0.0, columns[k])
                    columns[k] = kept - jnp.where(here, -entry, column * entry) * inverse
                else:
                    columns[k] = jnp.where(here, entry * inverse, columns[k] - column * (entry * inverse))
                under[k] = under[k] - under[p] * (entry * inverse)
            if hi < n:
                columns[p] = jnp.where(here, inverse, -column * inverse)
                under[p] = -under[p] * inverse
            else:
                for k in range(p + 1, 8):
                    entry = row_of(columns[k], p) * inverse
                    columns[k] = jnp.where(here, entry, columns[k] - column * entry)
        result[lo:hi, :] = jnp.where(lane <= sub + lo, scaled, 0.0)
        if hi < n:
            columns = [
                later[k] + total([under[p] * row_of(across[k], p) for p in range(8)])
                for k in range(8)
            ]
            lane_rest = lax.broadcasted_iota(jnp.int32, rest.shape, 1)
            kept = jnp.where((lane_rest >= lo) & (lane_rest < hi), 0.0, rest)
            work[hi:, :] = kept - total(
                [factors[k] * jnp.broadcast_to(rows[k : k + 1, :], rest.shape) for k in range(8)]
            )


def sweep_kernel(
    sweeps, place_ref, mine_ref, other_ref, start_ref, block_ref, blocks, gram_high, gram_low,
    ahead, work, factor,
):
    place = place_ref[0]
    part = mine_ref.shape[0] // 4
    for k in range(4):
        quarter = ((place >> 2) & 3) ^ k
        mine = pl.multiple_of(((place & 1) * 4 + quarter) * part, 8)
        theirs = pl.multiple_of(((1 - (place & 1)) * 4 + quarter) * part, 8)
        blocks[pl.ds(mine, part), :] = mine_ref[k * part : (k + 1) * part, :]
        blocks[pl.ds(theirs, part), :] = other_ref[k * part : (k + 1) * part, :]
    n = gram_high.shape[0]

    def place_block(i, j, block):
        gram_high[span(i), span(j)], gram_low[span(i), span(j)] = halves(block)

    above = upper_blocks(n)
    for number, (i, j) in enumerate(above):
        block = blocks[span(number), :]
        place_block(i, j, block)
        place_block(j, i, block.T)
    row, column = block_indices()
    tail = len(above) + n // EDGE // 2
    for pair in range(n // EDGE // 2):
        block = blocks[span(len(above) + pair), :]
        turned = block.T
        diagonal = blocks[tail * EDGE + pair : tail * EDGE + pair + 1, :]
        place_block(2 * pair, 2 * pair, jnp.where(row <= column, block, turned))
        second = jnp.where(row == column, diagonal, jnp.where(row > column, block, turned))
        place_block(2 * pair + 1, 2 * pair + 1, second)

    def by_gram(block):
        high, low = halves(block)
        both = dot(jnp.concatenate([high, low], axis=0), gram_high[...], NN)
        rank = block.shape[0]
        return both[:rank] + both[rank:] + dot(high, gram_low[...], NN)

    block_ref[...] = by_gram(start_ref[...].T)

    def sweep(_, carry):
        block = block_ref[...]
        work[...] = dot(block, block, NT, HIGHEST)
        ahead[...] = by_gram(block)
        invert_factor(work, factor)
        block_ref[...] = split_dot(factor[...], ahead[...])
        return carry

    lax.fori_loop(0, sweeps - 1, sweep, 0)


def iterate(place, mine, other, start):
    n, rank = start.shape
    vmem = pl.BlockSpec(memory_space=pltpu.VMEM)
    return pl.pallas_call(
        functools.partial(sweep_kernel, SWEEPS),
        in_specs=[pl.BlockSpec(memory_space=pltpu.SMEM), vmem, vmem, vmem],
        out_specs=vmem,
        out_shape=jax.ShapeDtypeStruct((rank, n), jnp.float32),
        scratch_shapes=[
            pltpu.VMEM((2 * mine.shape[0], 128), jnp.float32),
            pltpu.VMEM((n, n), jnp.bfloat16),
            pltpu.VMEM((n, n), jnp.bfloat16),
            pltpu.VMEM((rank, n), jnp.float32),
            pltpu.VMEM((rank, rank), jnp.float32),
            pltpu.VMEM((rank, rank), jnp.float32),
        ],
        cost_estimate=BRIEF,
        compiler_params=pltpu.CompilerParams(vmem_limit_bytes=16 * MIB),
        name="iterate",
    )(place, mine, other, start)


def factor_kernel(block_ref, out_ref, work):
    block = block_ref[...]
    work[...] = dot(block, block, NT, HIGHEST)
    invert_factor(work, out_ref)


def last_factor(block):
    rank = block.shape[0]
    vmem = pl.BlockSpec(memory_space=pltpu.VMEM)
    return pl.pallas_call(
        factor_kernel,
        in_specs=[vmem],
        out_specs=vmem,
        out_shape=jax.ShapeDtypeStruct((rank, rank), jnp.float32),
        scratch_shapes=[pltpu.VMEM((rank, rank), jnp.float32)],
        cost_estimate=BRIEF,
        compiler_params=pltpu.CompilerParams(vmem_limit_bytes=16 * MIB),
        name="last_factor",
    )(block)


def weights(block_ref):
    return jnp.concatenate(halves(block_ref[...]), axis=0)


def split_product(high, low, both):
    rank = both.shape[0] // 2
    product = dot(high, both, NT)
    return product[:, :rank] + product[:, rank:] + dot(low, both[:rank], NT)


def halved_product(x, both):
    return split_product(*halves(x), both)


def pick(held, place_ref, rank, first, fibres, j):
    start = first * 8 + (place_ref[1] ^ rank) * (8 // SLABS) + j
    return side_by_side(held, pl.ds(start, fibres, stride=8))


def chunks_of(rank):
    return sum(count for to, _, count in EARLY if to == rank)


def prepare_kernel(place_ref, held, *refs):
    per = 8 // SLABS
    high_ref, low_ref = refs[-2:]
    chunk = held.shape[1] // 8 // CHUNKS
    for (rank, first, count), out in zip(EARLY, refs[:-2], strict=True):
        for j in range(per):
            rows = pick(held, place_ref, rank, first * chunk, count * chunk, j)
            for c in range(out.shape[0]):
                out[c, pl.ds(j, count * chunk, stride=per), :] = rows[:, c * 128 : (c + 1) * 128]
    begin = 0
    for rank in (1, *FAR):
        first = chunks_of(rank) * chunk
        fibres = CHUNKS * chunk - first
        for j in range(per):
            high, low = halves(pick(held, place_ref, rank, first, fibres, j))
            high_ref[begin : begin + fibres, :] = high
            low_ref[begin : begin + fibres, :] = low
            begin += fibres


def prepare(place, held):
    columns, rows, lanes = held.shape
    chunk = rows // SLABS // CHUNKS
    count = sum(CHUNKS - chunks_of(rank) for rank in (1, *FAR)) * chunk
    split = jax.ShapeDtypeStruct((count, columns * lanes), jnp.bfloat16)
    sent = [
        jax.ShapeDtypeStruct((columns, some * chunk, lanes), jnp.float32) for _, _, some in EARLY
    ]
    vmem = pl.BlockSpec(memory_space=pltpu.VMEM)
    return pl.pallas_call(
        prepare_kernel,
        in_specs=[pl.BlockSpec(memory_space=pltpu.SMEM), vmem],
        out_specs=[vmem] * (len(sent) + 2),
        out_shape=[*sent, split, split],
        cost_estimate=BRIEF,
        compiler_params=pltpu.CompilerParams(vmem_limit_bytes=16 * MIB),
        name="prepare",
    )(place, held)


def sent_kernel(begin, groups, high_ref, low_ref, block_ref, *outs):
    per = 8 // SLABS
    both = weights(block_ref)
    outs = list(outs)
    for parts in groups:
        some = [outs.pop(0) for _ in range(parts)]
        fibres = sum(out.shape[0] for out in some) // per
        rows = slice(begin, begin + fibres * per)
        product = split_product(high_ref[rows, :], low_ref[rows, :], both)
        first = 0
        for out in some:
            count = out.shape[0] // per
            for j in range(per):
                start = j * fibres + first
                out[pl.ds(j, count, stride=per), :] = product[start : start + count]
            first += count
        begin += fibres * per


def project_sent(high, low, block, begin, groups, name):
    rank = block.shape[0]
    sizes = [size for group in groups for size in group]
    vmem = pl.BlockSpec(memory_space=pltpu.VMEM)
    return pl.pallas_call(
        functools.partial(sent_kernel, begin, [len(group) for group in groups]),
        in_specs=[vmem] * 3,
        out_specs=[vmem] * len(sizes),
        out_shape=[jax.ShapeDtypeStruct((size, rank), jnp.float32) for size in sizes],
        cost_estimate=BRIEF,
        compiler_params=pltpu.CompilerParams(vmem_limit_bytes=16 * MIB),
        name=name,
    )(high, low, block)


def own_kernel(place_ref, held, block_ref, out):
    per = 8 // SLABS
    both = weights(block_ref)
    fibres = held.shape[1] // 8
    x = jnp.concatenate([pick(held, place_ref, 0, 0, fibres, j) for j in range(per)], axis=0)
    product = halved_product(x, both)
    for j in range(per):
        out[pl.ds(j, fibres, stride=per), :] = product[j * fibres : (j + 1) * fibres]


def project_own(place, held, block):
    vmem = pl.BlockSpec(memory_space=pltpu.VMEM)
    return pl.pallas_call(
        own_kernel,
        in_specs=[pl.BlockSpec(memory_space=pltpu.SMEM), vmem, vmem],
        out_specs=vmem,
        out_shape=jax.ShapeDtypeStruct((held.shape[1] // SLABS, block.shape[0]), jnp.float32),
        cost_estimate=BRIEF,
        compiler_params=pltpu.CompilerParams(vmem_limit_bytes=16 * MIB),
        name="project_own",
    )(place, held, block)


def arrived_kernel(block_ref, *refs):
    outs = refs[-len(FAR) :]
    both = weights(block_ref)
    begins = [0] * len(FAR)
    for (rank, _, _), x_ref in zip(EARLY, refs[: len(EARLY)], strict=True):
        k, size = FAR.index(rank), x_ref.shape[1]
        x = side_by_side(x_ref, slice(None))
        outs[k][begins[k] : begins[k] + size, :] = halved_product(x, both)
        begins[k] += size


def project_arrived(block, arrived):
    vmem = pl.BlockSpec(memory_space=pltpu.VMEM)
    chunk = arrived[0].shape[1] // EARLY[0][2]
    return pl.pallas_call(
        arrived_kernel,
        in_specs=[vmem] * (1 + len(arrived)),
        out_specs=[vmem] * len(FAR),
        out_shape=[
            jax.ShapeDtypeStruct((chunks_of(rank) * chunk, block.shape[0]), jnp.float32)
            for rank in FAR
        ],
        cost_estimate=BRIEF,
        compiler_params=pltpu.CompilerParams(vmem_limit_bytes=16 * MIB),
        name="project_arrived",
    )(block, *arrived)


def finish_kernel(ranks, firsts, place_ref, factor_ref, *refs):
    pieces = refs[: len(ranks)]
    out, *results, sems = refs[-2 - len(ranks) :]
    both = weights(factor_ref)
    per, size = out.shape[2], out.shape[3]
    sends = []
    for k, (rank, first, piece) in enumerate(zip(ranks, firsts, pieces, strict=True)):
        last = first + results[k].shape[0]
        begin = first
        while begin < last:
            length = min(per - begin % per, last - begin)
            done = pl.ds(begin - first, length)
            rows = piece[(begin - first) * size : (begin - first + length) * size, :]
            results[k][done] = halved_product(rows, both).reshape(length, size, -1)
            send = pltpu.make_async_copy(
                results[k].at[done],
                out.at[begin // per, place_ref[1] ^ rank, pl.ds(begin % per, length)],
                sems.at[k, begin // per],
            )
            send.start()
            sends.append(send)
            begin += length
    for send in sends:
        send.wait()


def finish(place, factor, pieces, ranks, firsts, into, name):
    shape = into if isinstance(into, tuple) else into.shape
    size, rank = shape[3:]
    vmem = pl.BlockSpec(memory_space=pltpu.VMEM)
    in_specs = [pl.BlockSpec(memory_space=pltpu.SMEM)] + [vmem] * (1 + len(pieces))
    operands = [place, factor, *pieces]
    aliases = {}
    if not isinstance(into, tuple):
        aliases = {len(operands): 0}
        in_specs.append(pl.BlockSpec(memory_space=pl.ANY))
        operands.append(into)
    return pl.pallas_call(
        functools.partial(finish_kernel, ranks, firsts),
        in_specs=in_specs,
        out_specs=pl.BlockSpec(memory_space=pl.ANY),
        out_shape=jax.ShapeDtypeStruct(shape, jnp.float32),
        scratch_shapes=[
            pltpu.VMEM((piece.shape[0] // size, size, rank), jnp.float32) for piece in pieces
        ]
        + [pltpu.SemaphoreType.DMA((len(pieces), shape[0]))],
        input_output_aliases=aliases,
        cost_estimate=BRIEF,
        compiler_params=pltpu.CompilerParams(vmem_limit_bytes=16 * MIB),
        name=name,
    )(*operands)


def per_device(fields, start_basis):
    nv, n2, n3, n1 = fields.shape
    slabs = lax.axis_size("slab")
    slab = lax.axis_index("slab")
    place = jnp.stack([lax.axis_index("wide") * slabs + slab, slab]).astype(jnp.int32)
    rows = fields.reshape(-1, n1)
    count = float(rows.shape[0] * lax.axis_size("wide") * slabs)
    def to_far(some, ranks):
        return [exchange(x, "slab", rank) for x, rank in zip(some, ranks, strict=True)]

    def send(prepared):
        *sent, high, low = prepared
        ranks = [rank for rank, _, _ in EARLY]
        return [high, low], to_far(sent, ranks)

    keep, give, held = local_gram(place, rows, count)
    prepared = prepare(place, held)
    mine, other, (high, low), arrived = sum_gram(keep, give, prepared, send)
    block = iterate(place, mine, other, start_basis)

    block, *arrived = lax.optimization_barrier((block, *arrived))
    chunk = rows.shape[0] // SLABS // CHUNKS
    near_rows = CHUNKS * chunk
    far_rows = [[(CHUNKS - chunks_of(rank)) * chunk] for rank in FAR]
    far = project_sent(high, low, block, near_rows, far_rows, "project_far")
    block, far = lax.optimization_barrier((block, far))
    far = to_far(far, FAR)
    near = project_sent(high, low, block, 0, [[near_rows // 2] * 2], "project_near")
    near = [exchange(x, "slab", 1) for x in near]
    own = project_own(place, held, block)
    arrived = project_arrived(block, arrived)
    factor = last_factor(block)

    per = CHUNKS // nv
    out = (nv, slabs, per, n2 * n3 // slabs // per, block.shape[0])
    late = [chunks_of(rank) for rank in FAR]
    out = finish(place, factor, arrived, FAR, (0, 0), out, "finish_arrived")
    out = finish(place, factor, far[:1], FAR[:1], late[:1], out, "finish_first_far")
    out = finish(place, factor, [own, *near], (0, 1, 1), (0, 0, CHUNKS // 2), out, "finish_near")
    out = finish(place, factor, far[1:], FAR[1:], late[1:], out, "finish_last_far")
    return out.reshape(nv, n2 * slabs, n3 // slabs, out.shape[-1])


def solution(mesh):
    in_specs = (P(None, "slab", "wide", None), P())
    out_specs = P(None, None, ("wide", "slab"), None)
    return jax.shard_map(
        per_device, mesh=mesh, in_specs=in_specs, out_specs=out_specs, check_vma=False
    )
```
